512 devices in a mesh: ctx: 32 (over z, x_hi), head: 16 (over y, x_lo, core).
Axes of the slice: x: 4 (x_hi: 2, x_lo: 2; x = x_hi * 2 + x_lo), y: 4, z: 16, core: 2. Of those that a mesh axis runs over, the one named last changes fastest.
Arguments:
- queries: bfloat16 [4096, 4096], P('ctx', 'head'), may hold values from -5 to 5
- keys: bfloat16 [4096, 4096], P('ctx', 'head'), may hold values from -5 to 5
- values: bfloat16 [4096, 4096], P('ctx', 'head'), may hold values from -6 to 6
- episode: int32 [4096], P('ctx'), may hold values from 0 to 126, as said below
- out_weight: bfloat16 [4096, 4096], P('head'), may hold values from -1.5 to 1.5
- d_out: bfloat16 [4096, 4096], P(('ctx', 'head')), may hold values from -0.3984375 to 0.3984375
Outputs:
- mixed: bfloat16 [4096, 4096], P(('ctx', 'head'))
- d_queries: bfloat16 [4096, 4096], P('ctx', 'head')
- d_keys: bfloat16 [4096, 4096], P('ctx', 'head')
- d_values: bfloat16 [4096, 4096], P('ctx', 'head')
The draws below stay inside these ranges and needn't reach their ends.
Inputs may be any that keep to these rules, and one draw needn't show every extreme that they name: Episode numbers never fall as time rises; the episode of time step t is 0 for t < 64 and 2 * (t // 64) - 1 or 2 * (t // 64) otherwise (so each episode has 1 to 64 time steps, and episode 0 has exactly 64).
All inputs are finite; a program needn't handle non-finite values.
Results may differ from the reference program's by a relative error of at most 0.02.
Values may be sent and summed in bfloat16 or wider, within the bound.
No kernel may reach another device: no remote copies, remote signals or barrier semaphores. Data moves between devices by JAX's collectives and lax.ppermute only.
A program may use at most 64 MiB of HBM per device.

```python
import jax
import jax.numpy as jnp
from jax import lax

D = 4096
H = 32
HD = 128
TOK_DEV = 128
TOKENS = 4096
WINDOW_EPS = 64
MOST = 64
N_CTX = 32


def normal_rows(key, factor):
    return jnp.clip(factor * jax.random.normal(key, (TOKENS, H * HD), jnp.float32), -5.0, 5.0)


def draw_queries(key, part):
    key = jax.random.fold_in(key, 1)
    field = normal_rows(key, 1.0)
    return field.astype(jnp.bfloat16)


def draw_keys(key, part):
    key = jax.random.fold_in(key, 2)
    field = normal_rows(key, 2.0)
    return field.astype(jnp.bfloat16)


def draw_episode(key, part):
    key = jax.random.fold_in(key, 3)
    spans = TOKENS // MOST
    cuts = jax.random.randint(key, (spans,), 1, MOST).astype(jnp.int32)
    cuts = cuts.at[0].set(MOST)
    moments = jnp.arange(TOKENS, dtype=jnp.int32)
    span_of = moments // MOST
    offset = moments % MOST
    later = (offset >= cuts[span_of]).astype(jnp.int32)
    first = (span_of >= 1).astype(jnp.int32)
    by_time = 2 * span_of + later - first
    blocks = TOKENS // TOK_DEV
    half_rows = TOK_DEV // 2
    rows = jnp.arange(TOKENS, dtype=jnp.int32)
    holder = rows // TOK_DEV
    place_in = rows % TOK_DEV
    stamps = jnp.where(place_in < half_rows, holder * half_rows + place_in, (2 * blocks - 1 - holder) * half_rows + place_in - half_rows).astype(jnp.int32)
    return by_time[stamps].astype(jnp.int32)


def levels(key, dims, cuts, low, top_value):
    factor_of, own = 1.0, jax.random.fold_in(key, 6)
    for axis_at, blocks in cuts:
        heights = jnp.exp(jax.random.uniform(jax.random.fold_in(own, axis_at), (blocks,), jnp.float32, low / len(cuts), top_value / len(cuts)))
        factor_of = factor_of * jnp.repeat(heights, dims[axis_at] // blocks).reshape([-1 if axis == axis_at else 1 for axis in range(len(dims))])
    return factor_of


def centred(rng, dims, width, limit, cuts=(), held_as=jnp.bfloat16):
    result = jax.random.normal(rng, dims, jnp.float32) * width
    if len(cuts) > 0:
        result = levels(rng, dims, cuts, -0.22, 0.18) * result
    return jnp.clip(result, min=-limit, max=limit).astype(held_as)


def setup_inputs(seed: int = 0) -> dict:
    streams_of = jax.random.split(jax.random.key(seed), 7)
    queries = draw_queries(jax.random.fold_in(streams_of[6], 71), 0)
    keys = draw_keys(jax.random.fold_in(streams_of[6], 71), 0)
    values = centred(streams_of[2], (TOKENS, H * HD), 1.0, 6.0, ((0, 32), (1, 16)))
    episode = draw_episode(jax.random.fold_in(streams_of[6], 71), 0)
    out_weight = centred(streams_of[4], (H * HD, D), 0.25, 1.5, ((0, 16),))
    d_out = centred(streams_of[5], (TOKENS, D), 0.0625, 0.3984375, ((0, 512),))
    return dict(queries=queries, keys=keys, values=values, episode=episode, out_weight=out_weight, d_out=d_out)


floor_score = -1e30


def time_steps(rows):
    half_rows = TOK_DEV // 2
    holder = rows // TOK_DEV
    offset = rows % TOK_DEV
    return jnp.where(offset < half_rows, holder * half_rows + offset,
                     (2 * N_CTX - 1 - holder) * half_rows + offset - half_rows).astype(jnp.int32)


def reference(queries, keys, values, episode, out_weight, d_out):
    scale = HD ** -0.5
    d_attn = jnp.dot(d_out, out_weight.T, preferred_element_type=jnp.float32).astype(jnp.bfloat16)
    stamps = time_steps(jnp.arange(TOKENS, dtype=jnp.int32))
    visible = (stamps[None, :] <= stamps[:, None]) & (episode[:, None] - episode[None, :] < WINDOW_EPS)

    def split_heads(array):
        return array.reshape(TOKENS, H, HD).transpose(1, 0, 2)

    def merge_heads(array):
        return array.transpose(1, 0, 2).reshape(TOKENS, H * HD)

    def one_head(operands):
        q_head, k_head, v_head, da_head = operands
        scores = jnp.dot(q_head, k_head.T, preferred_element_type=jnp.float32) * scale
        scores = jnp.where(visible, scores, floor_score)
        top = jnp.max(scores, axis=1)
        lse = top + jnp.log(jnp.sum(jnp.exp(scores - top[:, None]), axis=1))
        probs = jnp.exp(scores - lse[:, None])
        probs_low = probs.astype(jnp.bfloat16)
        attn_head = jnp.dot(probs_low, v_head, preferred_element_type=jnp.float32).astype(jnp.bfloat16)
        delta = jnp.sum(da_head.astype(jnp.float32) * attn_head.astype(jnp.float32), axis=1)
        d_probs = jnp.dot(da_head, v_head.T, preferred_element_type=jnp.float32)
        d_scores = (probs * (d_probs - delta[:, None])).astype(jnp.bfloat16)
        dq_head = (scale * jnp.dot(d_scores, k_head, preferred_element_type=jnp.float32)).astype(jnp.bfloat16)
        dk_head = (scale * jnp.dot(d_scores.T, q_head, preferred_element_type=jnp.float32)).astype(jnp.bfloat16)
        dv_head = jnp.dot(probs_low.T, da_head, preferred_element_type=jnp.float32).astype(jnp.bfloat16)
        return attn_head, dq_head, dk_head, dv_head

    attn, d_queries, d_keys, d_values = lax.map(
        one_head, (split_heads(queries), split_heads(keys), split_heads(values), split_heads(d_attn)))
    mixed = jnp.dot(merge_heads(attn), out_weight, preferred_element_type=jnp.float32).astype(jnp.bfloat16)
    return mixed, merge_heads(d_queries), merge_heads(d_keys), merge_heads(d_values)
```

```python
import functools

import jax
import jax.numpy as jnp
from jax import lax
from jax.experimental import pallas as pl
from jax.experimental.pallas import tpu as pltpu
from jax.sharding import Mesh, PartitionSpec as P

HD = 128
ROWS = 128
HALF = ROWS // 2
GROUP = 8
CTX = 32
WINDOW = 2 * CTX
STAT = 16
LOG2E = 1.4426950408889634
SCALE = HD ** (-0.5)
FLOOR = -1e30

ZH, ZL, XH = "zh", "zl", "xh"
HEAD = ("y", "xl", "core")
Q_AXES = ("zl", "xh")
K_AXES = ("zh", "xh")

f32 = jnp.float32
bf16 = jnp.bfloat16


def q_block(pos_ref, s):
    return (pos_ref[0] * 4 + s // 2) * 2 + s % 2


def k_block(pos_ref, s):
    return ((s // 2) * 4 + pos_ref[1]) * 2 + s % 2


def time_of(block, offset):
    return jnp.where(
        offset < HALF, block * HALF + offset, (2 * CTX - 1 - block) * HALF + offset - HALF
    )


def split3(x):
    high = x.astype(bf16).astype(f32)
    rest = x - high
    mid = rest.astype(bf16).astype(f32)
    return high, mid, rest - mid


def stat_rows(a, b):
    row = lax.broadcasted_iota(jnp.int32, (STAT, ROWS), 0)
    out = jnp.zeros((STAT, ROWS), f32)
    for at, piece in enumerate(split3(a) + split3(b)):
        out = jnp.where(row == at, piece, out)
    return out.astype(bf16)


def stats_of(rows):
    rows = rows.astype(f32)
    return rows[0:1] + rows[1:2] + rows[2:3], rows[3:4] + rows[4:5] + rows[5:6]


def key_columns(pos_ref, kv_ref, s):
    offset = lax.broadcasted_iota(jnp.int32, (ROWS, ROWS), 0)
    times = time_of(k_block(pos_ref, s), offset)
    ep = kv_ref[s, 2 * ROWS : 2 * ROWS + STAT, :].astype(f32)[0:1]
    episodes = jnp.broadcast_to(ep, (ROWS, ROWS)).T
    return times, episodes


def query_rows(pos_ref, q_ref, s):
    offset = lax.broadcasted_iota(jnp.int32, (1, ROWS), 1)
    times = time_of(q_block(pos_ref, s), offset)
    ep = q_ref[s, ROWS : ROWS + STAT, :].astype(f32)[0:1]
    return times, ep - WINDOW


def pack_kernel(q_ref, k_ref, v_ref, ep_ref, qs_ref, kvs_ref):
    ep = jnp.broadcast_to(ep_ref[...].astype(f32), (STAT, ROWS)).astype(bf16)
    for s in range(GROUP):
        cols = slice((s % 2) * HD, (s % 2 + 1) * HD)
        qs_ref[s, 0:ROWS, :] = q_ref[:, cols]
        qs_ref[s, ROWS : ROWS + STAT, :] = ep
        kvs_ref[s, 0:ROWS, :] = k_ref[:, cols]
        kvs_ref[s, ROWS : 2 * ROWS, :] = v_ref[:, cols]
        kvs_ref[s, 2 * ROWS : 2 * ROWS + STAT, :] = ep


def forward_kernel(pos_ref, q_ref, kv_ref, os_ref, vt_ref, tk_ref, ek_ref):
    for s in range(GROUP):
        at = slice(s * ROWS, (s + 1) * ROWS)
        vt_ref[:, at] = kv_ref[s, ROWS : 2 * ROWS, :].T
        tk_ref[at, :], ek_ref[at, :] = key_columns(pos_ref, kv_ref, s)
    keys = kv_ref[:, 0:ROWS, :].reshape(GROUP * ROWS, HD)
    for s in range(0, GROUP, 2):
        qb = q_ref[s : s + 2, 0:ROWS, :].reshape(2 * ROWS, HD)
        st = lax.dot_general(keys, qb, (((1,), (1,)), ((), ())), preferred_element_type=f32)
        parts = []
        for u in range(2):
            tq, eq = query_rows(pos_ref, q_ref, s + u)
            seen = (tk_ref[...] <= tq) & (ek_ref[...] > eq)
            sc = jnp.where(seen, st[:, u * ROWS : (u + 1) * ROWS] * (SCALE * LOG2E), FLOOR)
            top = jnp.max(sc, axis=0, keepdims=True)
            p = jnp.exp2(sc - top)
            total = jnp.sum(p, axis=0, keepdims=True)
            parts.append(p.astype(bf16))
            os_ref[s + u, HD : HD + STAT, :] = stat_rows(top, total)
        o = jnp.dot(vt_ref[...], jnp.concatenate(parts, axis=1), preferred_element_type=f32)
        for u in range(2):
            os_ref[s + u, 0:HD, :] = o[:, u * ROWS : (u + 1) * ROWS].astype(bf16)


def combine_kernel(os_ref, da_ref, attn_ref, das_ref):
    for h in range(2):
        cols = slice(h * HD, (h + 1) * HD)
        stats = [stats_of(os_ref[2 * c + h, HD : HD + STAT, :]) for c in range(4)]
        top = functools.reduce(jnp.maximum, [m for m, _ in stats])
        weights = [jnp.exp2(m - top) for m, _ in stats]
        total = sum(w * t for w, (_, t) in zip(weights, stats))
        attn_t = sum(
            (w / total) * os_ref[2 * c + h, 0:HD, :].astype(f32) for c, w in enumerate(weights)
        )
        lse = top + jnp.log(total) * LOG2E
        low = attn_t.astype(bf16).astype(f32)
        attn_ref[:, cols] = low.T.astype(bf16)
        da = da_ref[:, cols]
        delta = jnp.sum(da.astype(f32).T * low, axis=0, keepdims=True)
        rows = stat_rows(lse, delta)
        for c in range(4):
            das_ref[2 * c + h, 0:ROWS, :] = da
            das_ref[2 * c + h, ROWS : ROWS + STAT, :] = rows


def backward_kernel(pos_ref, q_ref, kv_ref, das_ref, dqs_ref, dkvs_ref, dq_acc):
    total = GROUP * ROWS
    queries = q_ref[:, 0:ROWS, :].reshape(total, HD)
    d_attn = das_ref[:, 0:ROWS, :].reshape(total, HD)
    tq, eq, lse, delta = [], [], [], []
    for s in range(GROUP):
        t, e = query_rows(pos_ref, q_ref, s)
        a, b = stats_of(das_ref[s, ROWS : ROWS + STAT, :])
        tq.append(t)
        eq.append(e)
        lse.append(a)
        delta.append(b)
    for s in range(0, GROUP, 2):
        kb = kv_ref[s : s + 2, 0:ROWS, :].reshape(2 * ROWS, HD)
        vb = kv_ref[s : s + 2, ROWS : 2 * ROWS, :].reshape(2 * ROWS, HD)
        nt = (((1,), (1,)), ((), ()))
        st = lax.dot_general(kb, queries, nt, preferred_element_type=f32)
        dp = lax.dot_general(vb, d_attn, nt, preferred_element_type=f32)
        tk0, ek0 = key_columns(pos_ref, kv_ref, s)
        tk1, ek1 = key_columns(pos_ref, kv_ref, s + 1)
        tk = jnp.concatenate([tk0, tk1], axis=0)
        ek = jnp.concatenate([ek0, ek1], axis=0)
        p_low, ds_low = [], []
        for u in range(GROUP):
            at = slice(u * ROWS, (u + 1) * ROWS)
            seen = (tk <= tq[u]) & (ek > eq[u])
            p = jnp.where(seen, jnp.exp2(st[:, at] * (SCALE * LOG2E) - lse[u]), 0.0)
            p_low.append(p.astype(bf16))
            ds_low.append((p * (dp[:, at] - delta[u])).astype(bf16))
        probs = jnp.concatenate(p_low, axis=1)
        ds = jnp.concatenate(ds_low, axis=1)
        dv = jnp.dot(probs, d_attn, preferred_element_type=f32)
        dk = jnp.dot(ds, queries, preferred_element_type=f32)
        dq = jnp.dot(kb.T, ds, preferred_element_type=f32)
        if s == 0:
            dq_acc[...] = dq
        else:
            dq_acc[...] += dq
        for u in range(2):
            at = slice(u * ROWS, (u + 1) * ROWS)
            dkvs_ref[s + u, 0:ROWS, :] = dk[at].astype(bf16)
            dkvs_ref[s + u, ROWS : 2 * ROWS, :] = dv[at].astype(bf16)
    for s in range(GROUP):
        dqs_ref[s] = dq_acc[:, s * ROWS : (s + 1) * ROWS].astype(bf16)


def finish_kernel(dqs_ref, dkvs_ref, dq_ref, dk_ref, dv_ref):
    for h in range(2):
        cols = slice(h * HD, (h + 1) * HD)
        dq = sum(dqs_ref[2 * c + h].astype(f32) for c in range(4))
        dkv = sum(dkvs_ref[2 * c + h].astype(f32) for c in range(4))
        dq_ref[:, cols] = (dq * SCALE).T.astype(bf16)
        dk_ref[:, cols] = (dkv[0:ROWS] * SCALE).astype(bf16)
        dv_ref[:, cols] = dkv[ROWS : 2 * ROWS].astype(bf16)


VMEM = pl.BlockSpec(memory_space=pltpu.VMEM)
SMEM = pl.BlockSpec(memory_space=pltpu.SMEM)


def call(kernel, outs, args, scratch=(), flops=0, smem=0):
    moved = sum(a.size * a.dtype.itemsize for a in args) + sum(
        functools.reduce(lambda x, y: x * y, shape) * 2 for shape in outs
    )
    return pl.pallas_call(
        kernel,
        out_shape=[jax.ShapeDtypeStruct(shape, bf16) for shape in outs],
        in_specs=[SMEM] * smem + [VMEM] * (len(args) - smem),
        out_specs=[VMEM] * len(outs),
        scratch_shapes=list(scratch),
        compiler_params=pltpu.CompilerParams(vmem_limit_bytes=32 * 1024 * 1024),
        cost_estimate=pl.CostEstimate(flops=flops, bytes_accessed=moved, transcendentals=0),
    )(*args)


def on_device(queries, keys, values, episode, out_weight, d_out):
    rows, width = queries.shape
    total = GROUP * ROWS
    pos = jnp.stack([lax.axis_index(ZH), lax.axis_index(ZL)]).astype(jnp.int32)
    swap = functools.partial(lax.all_to_all, split_axis=0, concat_axis=0, tiled=True)
    d_out_all = lax.all_gather(d_out, HEAD, axis=0, tiled=True)
    q_slots, kv_slots = call(
        pack_kernel,
        [(GROUP, ROWS + STAT, HD), (GROUP, 2 * ROWS + STAT, HD)],
        (queries, keys, values, episode.reshape(1, rows)),
    )
    kv = swap(kv_slots, K_AXES)
    q = swap(q_slots, Q_AXES)
    (o_slots,) = call(
        forward_kernel,
        [(GROUP, HD + STAT, ROWS)],
        (pos, q, kv),
        [pltpu.VMEM((HD, total), bf16), pltpu.VMEM((total, ROWS), jnp.int32), pltpu.VMEM((total, ROWS), f32)],
        flops=4 * total * total * HD,
        smem=1,
    )
    o = swap(o_slots, Q_AXES)
    d_attn = lax.dot_general(
        d_out_all, out_weight, (((1,), (1,)), ((), ())), preferred_element_type=f32
    ).astype(bf16)
    attn, da_slots = call(
        combine_kernel, [(rows, width), (GROUP, ROWS + STAT, HD)], (o, d_attn)
    )
    partial = jnp.dot(attn, out_weight, preferred_element_type=f32)
    partial, da_slots = lax.optimization_barrier((partial, da_slots))
    mixed = lax.psum_scatter(partial, HEAD, scatter_dimension=0, tiled=True).astype(bf16)
    da = swap(da_slots, Q_AXES)
    dq_slots, dkv_slots = call(
        backward_kernel,
        [(GROUP, HD, ROWS), (GROUP, 2 * ROWS, HD)],
        (pos, q, kv, da),
        [pltpu.VMEM((HD, total), f32)],
        flops=10 * total * total * HD,
        smem=1,
    )
    dkv = swap(dkv_slots, K_AXES)
    dq = swap(dq_slots, Q_AXES)
    d_queries, d_keys, d_values = call(finish_kernel, [(rows, width)] * 3, (dq, dkv))
    return mixed, d_queries, d_keys, d_values


def solution(mesh):
    inner = Mesh(
        mesh.devices.reshape(4, 4, 2, 4, 2, 2), ("zh", "zl", "xh", "y", "xl", "core")
    )
    ctx = ("zh", "zl", "xh")
    block = P(ctx, HEAD)
    whole = P(ctx + HEAD, None)
    return jax.shard_map(
        on_device,
        mesh=inner,
        in_specs=(block, block, block, P(ctx), P(HEAD, None), whole),
        out_specs=(whole, block, block, block),
        check_vma=False,
    )
```

```python
import functools

import jax
import jax.numpy as jnp
from jax import lax
from jax.experimental import pallas as pl
from jax.experimental.pallas import tpu as pltpu
from jax.sharding import Mesh, PartitionSpec as P

HD = 128
ROWS = 128
HALF = ROWS // 2
PIECE = 32
SHARES = 32
PLANES = 16
CTX = 32
WINDOW = 2 * CTX
STAT = 16
LOG2E = 1.4426950408889634
SCALE = HD ** (-0.5)
FLOOR = -1e30

AXES = ("z", "xh", "y", "xl", "core")
HEAD = ("y", "xl", "core")
TURN = ("z",) + HEAD
PLANE = ("xh",) + HEAD
S_AXES = ("xh", "xl")

f32 = jnp.float32
bf16 = jnp.bfloat16
NT = (((1,), (1,)), ((), ()))


def slot_of(place):
    return place % 8 * 2 + place // 8


def place_of(slot):
    return slot // 2 + slot % 2 * 8


def share(xh, y, xl, core):
    return ((xh * 4 + y) * 2 + xl) * 2 + core


def times_of(row, piece, plane):
    source = row // PIECE
    place = source % 2 * 8 + source // 4 % 4 * 2 + source // 2 % 2
    block = (place - plane + PLANES) % PLANES * 2 + source // 16
    offset = row % PIECE + piece % 2 * PIECE
    return jnp.where(piece < 2, block, 2 * CTX - 1 - block) * HALF + offset


def episodes_of(x_ref, at, group):
    lane = lax.broadcasted_iota(jnp.int32, (1, ROWS), 1) // PIECE
    out = jnp.zeros((1, ROWS), f32)
    for u in range(4):
        rows = x_ref[4 * group + u, 4 * PIECE : 4 * PIECE + STAT, :].astype(f32)
        out = jnp.where(lane == u, rows[at : at + 1], out)
    return out


def key_columns(pos_ref, x_ref, group):
    row = lax.broadcasted_iota(jnp.int32, (ROWS, ROWS), 0) + group * ROWS
    times = times_of(row, pos_ref[2] * 2 + pos_ref[1], pos_ref[3])
    return times, jnp.broadcast_to(episodes_of(x_ref, 1, group), (ROWS, ROWS)).T


def query_rows(pos_ref, x_ref, group):
    row = lax.broadcasted_iota(jnp.int32, (1, ROWS), 1) + group * ROWS
    times = times_of(row, pos_ref[0], pos_ref[3])
    return times, episodes_of(x_ref, 0, group) - WINDOW


def part(x_ref, at, first=0, count=SHARES):
    return x_ref[first : first + count, at * PIECE : (at + 1) * PIECE, :].reshape(count * PIECE, HD)


def prepare_kernel(q_ref, k_ref, v_ref, ep_ref, d_ref, qkv_out, d_out, ep_buf, d_buf, sems):
    copies = [
        pltpu.make_async_copy(q_ref, qkv_out.at[0:ROWS], sems.at[0]),
        pltpu.make_async_copy(k_ref, qkv_out.at[ROWS : 2 * ROWS], sems.at[1]),
        pltpu.make_async_copy(v_ref, qkv_out.at[2 * ROWS : 3 * ROWS], sems.at[2]),
        pltpu.make_async_copy(d_ref, d_buf, sems.at[3]),
        pltpu.make_async_copy(ep_ref, ep_buf, sems.at[4]),
    ]
    for copy in copies:
        copy.start()
    for copy in copies:
        copy.wait()
    ep = jnp.broadcast_to(ep_buf[...].astype(f32), (STAT, ROWS)).astype(bf16)
    qkv_out[3 * ROWS : 3 * ROWS + STAT] = jnp.concatenate([ep, ep], axis=1)
    for s in range(PLANES):
        d_out[s] = d_buf[...]


def pack_kernel(qkv_ref, da_ref, out_ref):
    ep = qkv_ref[3 * ROWS : 3 * ROWS + STAT, 0:ROWS].astype(f32)
    tiled = []
    for piece in range(4):
        own = ep[:, piece * PIECE : (piece + 1) * PIECE]
        tiled.append(jnp.concatenate([own] * 4, axis=1))
    row = lax.broadcasted_iota(jnp.int32, (STAT, ROWS), 0)
    for xh in range(2):
        for y in range(4):
            for xl in range(2):
                x = xh * 2 + xl
                both = jnp.where(row == 0, tiled[y], tiled[x]).astype(bf16)
                for core in range(2):
                    s = share(xh, y, xl, core)
                    cols = slice(core * HD, (core + 1) * HD)
                    q_rows = slice(y * PIECE, (y + 1) * PIECE)
                    out_ref[s, 0:PIECE, :] = qkv_ref[q_rows, cols]
                    out_ref[s, PIECE : 2 * PIECE, :] = da_ref[q_rows, cols]
                    for at in (1, 2):
                        k_rows = slice(at * ROWS + x * PIECE, at * ROWS + (x + 1) * PIECE)
                        out_ref[s, (at + 1) * PIECE : (at + 2) * PIECE, :] = qkv_ref[k_rows, cols]
                    out_ref[s, 4 * PIECE : 4 * PIECE + STAT, :] = both


def totals_kernel(pos_ref, x_ref, stat_ref, tk_ref, ek_ref):
    for g in range(8):
        at = slice(g * ROWS, (g + 1) * ROWS)
        tk_ref[at, :], ek_ref[at, :] = key_columns(pos_ref, x_ref, g)
    keys, values = part(x_ref, 2), part(x_ref, 3)
    row = lax.broadcasted_iota(jnp.int32, (8, ROWS), 0)
    for g in range(0, 8, 2):
        qb, db = part(x_ref, 0, 4 * g, 8), part(x_ref, 1, 4 * g, 8)
        st = lax.dot_general(keys, qb, NT, preferred_element_type=f32)
        dp = lax.dot_general(values, db, NT, preferred_element_type=f32)
        for u in range(2):
            tq, eq = query_rows(pos_ref, x_ref, g + u)
            at = slice(u * ROWS, (u + 1) * ROWS)
            seen = (tk_ref[...] <= tq) & (ek_ref[...] > eq)
            sc = jnp.where(seen, st[:, at] * (SCALE * LOG2E), FLOOR)
            top = jnp.max(sc, axis=0, keepdims=True)
            p = jnp.exp2(sc - top)
            total = jnp.sum(p, axis=0, keepdims=True)
            inner = jnp.sum(p * dp[:, at], axis=0, keepdims=True)
            rows = jnp.where(row == 0, top, jnp.where(row == 1, total, jnp.where(row == 2, inner, 0.0)))
            for c in range(4):
                stat_ref[c, :, (g + u) * ROWS : (g + u + 1) * ROWS] = rows


def backward_kernel(pos_ref, x_ref, stat_ref, oq_ref, grad_ref, dq_acc, o_acc):
    queries, d_attn = part(x_ref, 0), part(x_ref, 1)
    tops = [stat_ref[c, 0:1, :] for c in range(4)]
    top = functools.reduce(jnp.maximum, tops)
    weights = [jnp.exp2(t - top) for t in tops]
    norm = sum(w * stat_ref[c, 1:2, :] for c, w in enumerate(weights))
    lse = top + jnp.log(norm) * LOG2E
    delta = sum(w * stat_ref[c, 2:3, :] for c, w in enumerate(weights)) / norm
    rows = [query_rows(pos_ref, x_ref, g) for g in range(8)]
    for g in range(0, 8, 2):
        kb, vb = part(x_ref, 2, 4 * g, 8), part(x_ref, 3, 4 * g, 8)
        st = lax.dot_general(kb, queries, NT, preferred_element_type=f32)
        dp = lax.dot_general(vb, d_attn, NT, preferred_element_type=f32)
        tk0, ek0 = key_columns(pos_ref, x_ref, g)
        tk1, ek1 = key_columns(pos_ref, x_ref, g + 1)
        tk = jnp.concatenate([tk0, tk1], axis=0)
        ek = jnp.concatenate([ek0, ek1], axis=0)
        p_low, ds_low = [], []
        for u in range(8):
            at = slice(u * ROWS, (u + 1) * ROWS)
            tq, eq = rows[u]
            seen = (tk <= tq) & (ek > eq)
            p = jnp.where(seen, jnp.exp2(st[:, at] * (SCALE * LOG2E) - lse[:, at]), 0.0)
            p_low.append(p.astype(bf16))
            ds_low.append((p * (dp[:, at] - delta[:, at])).astype(bf16))
        probs = jnp.concatenate(p_low, axis=1)
        ds = jnp.concatenate(ds_low, axis=1)
        dv = jnp.dot(probs, d_attn, preferred_element_type=f32)
        dk = jnp.dot(ds, queries, preferred_element_type=f32)
        dq = jnp.dot(kb.T, ds, preferred_element_type=f32)
        o = jnp.dot(vb.T, probs, preferred_element_type=f32)
        if g == 0:
            dq_acc[...] = dq
            o_acc[...] = o
        else:
            dq_acc[...] += dq
            o_acc[...] += o
        for at, grad in ((0, dk), (1, dv)):
            grad_ref[4 * g : 4 * g + 8, at * PIECE : (at + 1) * PIECE, :] = grad.astype(
                bf16
            ).reshape(8, PIECE, HD)
    for g in range(8):
        at = slice(g * ROWS, (g + 1) * ROWS)
        four = slice(4 * g, 4 * g + 4)
        oq_ref[four, PIECE : 2 * PIECE, :] = dq_acc[:, at].T.astype(bf16).reshape(4, PIECE, HD)
        oq_ref[four, 0:PIECE, :] = o_acc[:, at].T.astype(bf16).reshape(4, PIECE, HD)


def queries_kernel(oq_ref, out_ref):
    for core in range(2):
        cols = slice(core * HD, (core + 1) * HD)
        for y in range(4):
            both = sum(oq_ref[share(x // 2, y, x % 2, core)].astype(f32) for x in range(4))
            rows = slice(y * PIECE, (y + 1) * PIECE)
            out_ref[rows, cols] = both[:PIECE].astype(bf16)
            rows = slice(ROWS + y * PIECE, ROWS + (y + 1) * PIECE)
            out_ref[rows, cols] = (both[PIECE:] * SCALE).astype(bf16)


def keys_kernel(grad_ref, out_ref):
    for core in range(2):
        cols = slice(core * HD, (core + 1) * HD)
        for x in range(4):
            both = sum(grad_ref[share(x // 2, y, x % 2, core)].astype(f32) for y in range(4))
            rows = slice(x * PIECE, (x + 1) * PIECE)
            out_ref[rows, cols] = (both[:PIECE] * SCALE).astype(bf16)
            rows = slice(ROWS + x * PIECE, ROWS + (x + 1) * PIECE)
            out_ref[rows, cols] = both[PIECE:].astype(bf16)


VMEM = pl.BlockSpec(memory_space=pltpu.VMEM)
SMEM = pl.BlockSpec(memory_space=pltpu.SMEM)


HBM = pl.BlockSpec(memory_space=pltpu.HBM)


def call(kernel, outs, args, scratch=(), flops=0, smem=0, space=VMEM, limit=32):
    size = lambda a: functools.reduce(lambda x, y: x * y, a.shape) * a.dtype.itemsize
    return pl.pallas_call(
        kernel,
        out_shape=outs,
        in_specs=[SMEM] * smem + [space] * (len(args) - smem),
        out_specs=[VMEM] * len(outs),
        scratch_shapes=list(scratch),
        compiler_params=pltpu.CompilerParams(vmem_limit_bytes=limit * 1024 * 1024),
        cost_estimate=pl.CostEstimate(
            flops=flops, bytes_accessed=sum(map(size, (*args, *outs))), transcendentals=0
        ),
    )(*args)


def turns():
    inside, across, there = [], [], []
    for z in range(PLANES):
        for g in range(PLANES):
            plane = place_of(g)
            at = slot_of((plane + z) % PLANES)
            inside.append((z * PLANES + g, z * PLANES + at))
            across.append((z * PLANES + at, plane * PLANES + at))
            there.append((z * PLANES + g, plane * PLANES + at))
    return inside, across, there, [(b, a) for a, b in there]


def on_device(queries, keys, values, episode, out_weight, d_out):
    rows, width = queries.shape
    total = SHARES * PIECE
    inside, across, there, back = turns()
    move = lambda x, pairs: lax.ppermute(x, TURN, pairs)
    swap = functools.partial(lax.all_to_all, split_axis=0, concat_axis=0, tiled=True)
    low = lambda *shape: jax.ShapeDtypeStruct(shape, bf16)
    pos = jnp.stack([lax.axis_index(a) for a in ("y", "xl", "xh", "z")]).astype(jnp.int32)
    qkv, d_slots = call(
        prepare_kernel,
        [low(3 * rows + STAT, width), low(PLANES, *d_out.shape)],
        (queries, keys, values, episode.reshape(1, rows), d_out),
        [
            pltpu.VMEM((1, rows), jnp.int32),
            pltpu.VMEM(d_out.shape, bf16),
            pltpu.SemaphoreType.DMA((5,)),
        ],
        space=HBM,
        limit=60,
    )
    qkv, d_slots = lax.optimization_barrier((move(qkv, inside), d_slots))
    qkv = move(qkv, across)
    d_out_all = swap(d_slots, HEAD)
    d_attn = lax.dot_general(
        d_out_all.reshape(rows, -1), out_weight, NT, preferred_element_type=f32
    ).astype(bf16)
    d_attn = move(d_attn, there)
    (slots,) = call(pack_kernel, [low(SHARES, 4 * PIECE + STAT, HD)], (qkv, d_attn))
    held = swap(slots, PLANE)
    (stats,) = call(
        totals_kernel,
        [jax.ShapeDtypeStruct((4, 8, total), f32)],
        (pos, held),
        [pltpu.VMEM((total, ROWS), jnp.int32), pltpu.VMEM((total, ROWS), f32)],
        flops=4 * total * total * HD,
        smem=1,
    )
    stats = swap(stats, S_AXES)
    oq_slots, grad_slots = call(
        backward_kernel,
        [low(SHARES, 2 * PIECE, HD), low(SHARES, 2 * PIECE, HD)],
        (pos, held, stats),
        [pltpu.VMEM((HD, total), f32)] * 2,
        flops=12 * total * total * HD,
        smem=1,
    )
    (own_q,) = call(queries_kernel, [low(2 * rows, width)], (swap(oq_slots, PLANE),))
    own_q = move(own_q, back)
    grad_parts, own_q = lax.optimization_barrier((swap(grad_slots, PLANE), own_q))
    (own_k,) = call(keys_kernel, [low(2 * rows, width)], (grad_parts,))
    own_k = move(own_k, back)
    partial = jnp.dot(own_q[:rows], out_weight, preferred_element_type=f32).astype(bf16)
    parts = swap(partial.reshape((PLANES,) + d_out.shape), HEAD)
    mixed = jnp.sum(parts.astype(f32), axis=0).astype(bf16)
    return mixed, own_q[rows:], own_k[:rows], own_k[rows:]


def solution(mesh):
    inner = Mesh(mesh.devices.reshape(16, 2, 4, 2, 2), AXES)
    ctx = ("z", "xh")
    block = P(ctx, HEAD)
    whole = P(ctx + HEAD, None)
    return jax.shard_map(
        on_device,
        mesh=inner,
        in_specs=(block, block, block, P(ctx), P(HEAD, None), whole),
        out_specs=(whole, block, block, block),
        check_vma=False,
    )
```

```python
import functools

import jax
import jax.numpy as jnp
from jax import lax
from jax.experimental import pallas as pl
from jax.experimental.pallas import tpu as pltpu
from jax.sharding import Mesh, PartitionSpec as P

HD = 128
ROWS = 128
HALF = ROWS // 2
PIECE = 32
SHARES = 32
PLANES = 16
CTX = 32
WINDOW = 2 * CTX
STAT = 16
LOG2E = 1.4426950408889634
SCALE = HD ** (-0.5)
FLOOR = -1e30

AXES = ("z", "xh", "y", "xl", "core")
HEAD = ("y", "xl", "core")
TURN = ("z",) + HEAD
PLANE = ("xh",) + HEAD

f32 = jnp.float32
bf16 = jnp.bfloat16
NT = (((1,), (1,)), ((), ()))


def slot_of(place):
    return place % 8 * 2 + place // 8


def place_of(slot):
    return slot // 2 + slot % 2 * 8


def share(xh, y, xl, core):
    return ((xh * 4 + y) * 2 + xl) * 2 + core


def times_of(row, piece, plane):
    source = row // PIECE
    place = source % 2 * 8 + source // 4 % 4 * 2 + source // 2 % 2
    block = (place - plane + PLANES) % PLANES * 2 + source // 16
    offset = row % PIECE + piece % 2 * PIECE
    return jnp.where(piece < 2, block, 2 * CTX - 1 - block) * HALF + offset


def episodes_of(x_ref, at, group):
    lane = lax.broadcasted_iota(jnp.int32, (1, ROWS), 1) // PIECE
    out = jnp.zeros((1, ROWS), f32)
    for u in range(4):
        rows = x_ref[4 * group + u, 3 * PIECE : 3 * PIECE + STAT, :].astype(f32)
        out = jnp.where(lane == u, rows[at : at + 1], out)
    return out


def split3(x):
    high = x.astype(bf16).astype(f32)
    rest = x - high
    mid = rest.astype(bf16).astype(f32)
    return high, mid, rest - mid


def stat_rows(a, b):
    row = lax.broadcasted_iota(jnp.int32, (STAT, ROWS), 0)
    out = jnp.zeros((STAT, ROWS), f32)
    for at, piece in enumerate(split3(a) + split3(b)):
        out = jnp.where(row == at, piece, out)
    return out


def stats_of(rows):
    return rows[0:1] + rows[1:2] + rows[2:3], rows[3:4] + rows[4:5] + rows[5:6]


def tile(rows, at):
    own = rows[:, at * PIECE : (at + 1) * PIECE]
    return jnp.concatenate([own] * 4, axis=1).astype(bf16)


def merge(pieces):
    lane = lax.broadcasted_iota(jnp.int32, (STAT, ROWS), 1) // PIECE
    out = jnp.zeros((STAT, ROWS), f32)
    for u, piece in enumerate(pieces):
        out = jnp.where(lane == u, piece.astype(f32), out)
    return out


def key_columns(pos_ref, x_ref, group):
    row = lax.broadcasted_iota(jnp.int32, (ROWS, ROWS), 0) + group * ROWS
    times = times_of(row, pos_ref[2] * 2 + pos_ref[1], pos_ref[3])
    return times, jnp.broadcast_to(episodes_of(x_ref, 1, group), (ROWS, ROWS)).T


def query_rows(pos_ref, x_ref, group):
    row = lax.broadcasted_iota(jnp.int32, (1, ROWS), 1) + group * ROWS
    times = times_of(row, pos_ref[0], pos_ref[3])
    return times, episodes_of(x_ref, 0, group) - WINDOW


def part(x_ref, at, first=0, count=SHARES):
    return x_ref[first : first + count, at * PIECE : (at + 1) * PIECE, :].reshape(count * PIECE, HD)


def prepare_kernel(q_ref, k_ref, v_ref, ep_ref, qkv_out, ep_buf, sems):
    copies = [
        pltpu.make_async_copy(q_ref, qkv_out.at[0:ROWS], sems.at[0]),
        pltpu.make_async_copy(k_ref, qkv_out.at[ROWS : 2 * ROWS], sems.at[1]),
        pltpu.make_async_copy(v_ref, qkv_out.at[2 * ROWS : 3 * ROWS], sems.at[2]),
        pltpu.make_async_copy(ep_ref, ep_buf, sems.at[3]),
    ]
    for copy in copies:
        copy.start()
    for copy in copies:
        copy.wait()
    ep = jnp.broadcast_to(ep_buf[...].astype(f32), (STAT, ROWS)).astype(bf16)
    qkv_out[3 * ROWS : 3 * ROWS + STAT] = jnp.concatenate([ep, ep], axis=1)


def repeat_kernel(d_ref, d_out, d_buf, sem):
    copy = pltpu.make_async_copy(d_ref, d_buf, sem)
    copy.start()
    copy.wait()
    for s in range(PLANES):
        d_out[s] = d_buf[...]


def pack_kernel(qkv_ref, out_ref):
    ep = qkv_ref[3 * ROWS : 3 * ROWS + STAT, 0:ROWS].astype(f32)
    tiled = []
    for piece in range(4):
        own = ep[:, piece * PIECE : (piece + 1) * PIECE]
        tiled.append(jnp.concatenate([own] * 4, axis=1))
    row = lax.broadcasted_iota(jnp.int32, (STAT, ROWS), 0)
    for xh in range(2):
        for y in range(4):
            for xl in range(2):
                x = xh * 2 + xl
                both = jnp.where(row == 0, tiled[y], tiled[x]).astype(bf16)
                for core in range(2):
                    s = share(xh, y, xl, core)
                    cols = slice(core * HD, (core + 1) * HD)
                    q_rows = slice(y * PIECE, (y + 1) * PIECE)
                    out_ref[s, 0:PIECE, :] = qkv_ref[q_rows, cols]
                    for at in (1, 2):
                        k_rows = slice(at * ROWS + x * PIECE, at * ROWS + (x + 1) * PIECE)
                        out_ref[s, at * PIECE : (at + 1) * PIECE, :] = qkv_ref[k_rows, cols]
                    out_ref[s, 3 * PIECE : 3 * PIECE + STAT, :] = both


def forward_kernel(pos_ref, x_ref, o_ref, tk_ref, ek_ref, vt_ref):
    for g in range(8):
        at = slice(g * ROWS, (g + 1) * ROWS)
        tk_ref[at, :], ek_ref[at, :] = key_columns(pos_ref, x_ref, g)
        vt_ref[:, at] = part(x_ref, 2, 4 * g, 4).T
    keys = part(x_ref, 1)
    for g in range(0, 8, 2):
        qb = part(x_ref, 0, 4 * g, 8)
        st = lax.dot_general(keys, qb, NT, preferred_element_type=f32)
        low = []
        for u in range(2):
            tq, eq = query_rows(pos_ref, x_ref, g + u)
            at = slice(u * ROWS, (u + 1) * ROWS)
            seen = (tk_ref[...] <= tq) & (ek_ref[...] > eq)
            sc = jnp.where(seen, st[:, at] * (SCALE * LOG2E), FLOOR)
            top = jnp.max(sc, axis=0, keepdims=True)
            p = jnp.exp2(sc - top)
            rows = stat_rows(top, jnp.sum(p, axis=0, keepdims=True))
            low.append(p.astype(bf16))
            for j in range(4):
                o_ref[4 * (g + u) + j, PIECE : PIECE + STAT, :] = tile(rows, j)
        o = jnp.dot(vt_ref[...], jnp.concatenate(low, axis=1), preferred_element_type=f32)
        for u in range(2):
            four = slice(4 * (g + u), 4 * (g + u) + 4)
            out = o[:, u * ROWS : (u + 1) * ROWS].T.astype(bf16)
            o_ref[four, 0:PIECE, :] = out.reshape(4, PIECE, HD)


def combine_kernel(o_ref, da_ref, attn_ref, das_ref):
    for core in range(2):
        cols = slice(core * HD, (core + 1) * HD)
        tops, sums, parts = [], [], []
        for x in range(4):
            slots = [share(x // 2, y, x % 2, core) for y in range(4)]
            top, total = stats_of(merge([o_ref[s, PIECE : PIECE + STAT, :] for s in slots]))
            tops.append(top)
            sums.append(total)
            parts.append(jnp.concatenate([o_ref[s, 0:PIECE, :] for s in slots], axis=0).astype(f32))
        top = functools.reduce(jnp.maximum, tops)
        weights = [jnp.exp2(t - top) for t in tops]
        total = sum(w * t for w, t in zip(weights, sums))
        low = sum(
            jnp.broadcast_to(w / total, (ROWS, ROWS)).T * o for w, o in zip(weights, parts)
        ).astype(bf16)
        attn_ref[:, cols] = low
        da = da_ref[:, cols]
        delta = jnp.sum((da.astype(f32) * low.astype(f32)).T, axis=0, keepdims=True)
        rows = stat_rows(top + jnp.log(total) * LOG2E, delta)
        for y in range(4):
            own = tile(rows, y)
            for x in range(4):
                s = share(x // 2, y, x % 2, core)
                das_ref[s, 0:PIECE, :] = da[y * PIECE : (y + 1) * PIECE]
                das_ref[s, PIECE : PIECE + STAT, :] = own


def backward_kernel(pos_ref, x_ref, d_ref, grad_ref, dq_acc):
    queries, d_attn = part(x_ref, 0), part(d_ref, 0)
    rows, stats = [], []
    for g in range(8):
        rows.append(query_rows(pos_ref, x_ref, g))
        stats.append(
            stats_of(merge([d_ref[4 * g + u, PIECE : PIECE + STAT, :] for u in range(4)]))
        )
    for g in range(0, 8, 2):
        kb, vb = part(x_ref, 1, 4 * g, 8), part(x_ref, 2, 4 * g, 8)
        st = lax.dot_general(kb, queries, NT, preferred_element_type=f32)
        dp = lax.dot_general(vb, d_attn, NT, preferred_element_type=f32)
        tk0, ek0 = key_columns(pos_ref, x_ref, g)
        tk1, ek1 = key_columns(pos_ref, x_ref, g + 1)
        tk = jnp.concatenate([tk0, tk1], axis=0)
        ek = jnp.concatenate([ek0, ek1], axis=0)
        p_low, ds_low = [], []
        for u in range(8):
            at = slice(u * ROWS, (u + 1) * ROWS)
            (tq, eq), (lse, delta) = rows[u], stats[u]
            seen = (tk <= tq) & (ek > eq)
            p = jnp.where(seen, jnp.exp2(st[:, at] * (SCALE * LOG2E) - lse), 0.0)
            p_low.append(p.astype(bf16))
            ds_low.append((p * (dp[:, at] - delta)).astype(bf16))
        probs = jnp.concatenate(p_low, axis=1)
        ds = jnp.concatenate(ds_low, axis=1)
        dv = jnp.dot(probs, d_attn, preferred_element_type=f32)
        dk = jnp.dot(ds, queries, preferred_element_type=f32)
        dq = jnp.dot(kb.T, ds, preferred_element_type=f32)
        if g == 0:
            dq_acc[...] = dq
        else:
            dq_acc[...] += dq
        for at, grad in ((1, dk), (2, dv)):
            grad_ref[4 * g : 4 * g + 8, at * PIECE : (at + 1) * PIECE, :] = grad.astype(
                bf16
            ).reshape(8, PIECE, HD)
    for g in range(8):
        at = slice(g * ROWS, (g + 1) * ROWS)
        four = slice(4 * g, 4 * g + 4)
        grad_ref[four, 0:PIECE, :] = dq_acc[:, at].T.astype(bf16).reshape(4, PIECE, HD)


def grads_kernel(grad_ref, out_ref):
    for core in range(2):
        cols = slice(core * HD, (core + 1) * HD)
        for i in range(4):
            over_x = [grad_ref[share(x // 2, i, x % 2, core), 0:PIECE].astype(f32) for x in range(4)]
            rows = slice(i * PIECE, (i + 1) * PIECE)
            out_ref[rows, cols] = (sum(over_x) * SCALE).astype(bf16)
            over_y = [grad_ref[share(i // 2, y, i % 2, core), PIECE:].astype(f32) for y in range(4)]
            both = sum(over_y)
            rows = slice(ROWS + i * PIECE, ROWS + (i + 1) * PIECE)
            out_ref[rows, cols] = (both[:PIECE] * SCALE).astype(bf16)
            rows = slice(2 * ROWS + i * PIECE, 2 * ROWS + (i + 1) * PIECE)
            out_ref[rows, cols] = both[PIECE:].astype(bf16)


VMEM = pl.BlockSpec(memory_space=pltpu.VMEM)
SMEM = pl.BlockSpec(memory_space=pltpu.SMEM)


HBM = pl.BlockSpec(memory_space=pltpu.HBM)


def call(kernel, outs, args, scratch=(), flops=0, smem=0, space=VMEM, limit=32):
    size = lambda a: functools.reduce(lambda x, y: x * y, a.shape) * a.dtype.itemsize
    return pl.pallas_call(
        kernel,
        out_shape=outs,
        in_specs=[SMEM] * smem + [space] * (len(args) - smem),
        out_specs=[VMEM] * len(outs),
        scratch_shapes=list(scratch),
        compiler_params=pltpu.CompilerParams(vmem_limit_bytes=limit * 1024 * 1024),
        cost_estimate=pl.CostEstimate(
            flops=flops, bytes_accessed=sum(map(size, (*args, *outs))), transcendentals=0
        ),
    )(*args)


def turns():
    inside, across, there = [], [], []
    for z in range(PLANES):
        for g in range(PLANES):
            plane = place_of(g)
            at = slot_of((plane + z) % PLANES)
            inside.append((z * PLANES + g, z * PLANES + at))
            across.append((z * PLANES + at, plane * PLANES + at))
            there.append((z * PLANES + g, plane * PLANES + at))
    return inside, across, there, [(b, a) for a, b in there]


def on_device(queries, keys, values, episode, out_weight, d_out):
    rows, width = queries.shape
    total = SHARES * PIECE
    inside, across, there, back = turns()
    move = lambda x, pairs: lax.ppermute(x, TURN, pairs)
    swap = functools.partial(lax.all_to_all, split_axis=0, concat_axis=0, tiled=True)
    low = lambda *shape: jax.ShapeDtypeStruct(shape, bf16)
    pos = jnp.stack([lax.axis_index(a) for a in ("y", "xl", "xh", "z")]).astype(jnp.int32)
    (qkv,) = call(
        prepare_kernel,
        [low(3 * rows + STAT, width)],
        (queries, keys, values, episode.reshape(1, rows)),
        [pltpu.VMEM((1, rows), jnp.int32), pltpu.SemaphoreType.DMA((4,))],
        space=HBM,
        limit=60,
    )
    (d_slots,) = call(
        repeat_kernel,
        [low(PLANES, *d_out.shape)],
        (d_out,),
        [pltpu.VMEM(d_out.shape, bf16), pltpu.SemaphoreType.DMA],
        space=HBM,
        limit=60,
    )
    qkv, d_slots = lax.optimization_barrier((move(qkv, inside), d_slots))
    qkv = move(qkv, across)
    d_out_all = swap(d_slots, HEAD)
    d_attn = lax.dot_general(
        d_out_all.reshape(rows, -1), out_weight, NT, preferred_element_type=f32
    ).astype(bf16)
    qkv, d_attn = lax.optimization_barrier((qkv, d_attn))
    d_attn = move(d_attn, there)
    (slots,) = call(pack_kernel, [low(SHARES, 3 * PIECE + STAT, HD)], (qkv,))
    held = swap(slots, PLANE)
    (o_slots,) = call(
        forward_kernel,
        [low(SHARES, PIECE + STAT, HD)],
        (pos, held),
        [
            pltpu.VMEM((total, ROWS), jnp.int32),
            pltpu.VMEM((total, ROWS), f32),
            pltpu.VMEM((HD, total), bf16),
        ],
        flops=4 * total * total * HD,
        smem=1,
    )
    o_slots, d_attn = lax.optimization_barrier((o_slots, d_attn))
    attn, da_slots = call(
        combine_kernel,
        [low(rows, width), low(SHARES, PIECE + STAT, HD)],
        (swap(o_slots, PLANE), d_attn),
    )
    attn = move(attn, back)
    (grad_slots,) = call(
        backward_kernel,
        [low(SHARES, 3 * PIECE, HD)],
        (pos, held, swap(da_slots, PLANE)),
        [pltpu.VMEM((HD, total), f32)],
        flops=10 * total * total * HD,
        smem=1,
    )
    grad_parts, attn = lax.optimization_barrier((swap(grad_slots, PLANE), attn))
    (grads,) = call(grads_kernel, [low(3 * rows, width)], (grad_parts,))
    grads = move(grads, back)
    partial = jnp.dot(attn, out_weight, preferred_element_type=f32).astype(bf16)
    parts = swap(partial.reshape((PLANES,) + d_out.shape), HEAD)
    mixed = jnp.sum(parts.astype(f32), axis=0).astype(bf16)
    return mixed, grads[:rows], grads[rows : 2 * rows], grads[2 * rows :]


def solution(mesh):
    inner = Mesh(mesh.devices.reshape(16, 2, 4, 2, 2), AXES)
    ctx = ("z", "xh")
    block = P(ctx, HEAD)
    whole = P(ctx + HEAD, None)
    return jax.shard_map(
        on_device,
        mesh=inner,
        in_specs=(block, block, block, P(ctx), P(HEAD, None), whole),
        out_specs=(whole, block, block, block),
        check_vma=False,
    )
```

```python
import functools

import jax
import jax.numpy as jnp
from jax import lax
from jax.experimental import pallas as pl
from jax.experimental.pallas import tpu as pltpu
from jax.sharding import Mesh, PartitionSpec as P

HD = 128
ROWS = 128
HALF = ROWS // 2
PIECE = 32
SHARES = 32
PLANES = 16
CTX = 32
WINDOW = 2 * CTX
STAT = 16
LOG2E = 1.4426950408889634
SCALE = HD ** (-0.5)
FLOOR = -1e30

AXES = ("z", "xh", "y", "xl", "core")
HEAD = ("y", "xl", "core")
TURN = ("z",) + HEAD
PLANE = ("xh",) + HEAD

f32 = jnp.float32
bf16 = jnp.bfloat16
NT = (((1,), (1,)), ((), ()))


def slot_of(place):
    return place % 8 * 2 + place // 8


def place_of(slot):
    return slot // 2 + slot % 2 * 8


def share(xh, y, xl, core):
    return ((xh * 4 + y) * 2 + xl) * 2 + core


def times_of(row, piece, plane):
    source = row // PIECE
    place = source % 2 * 8 + source // 4 % 4 * 2 + source // 2 % 2
    block = (place ^ plane) * 2 + source // 16
    offset = row % PIECE + piece % 2 * PIECE
    return jnp.where(piece < 2, block, 2 * CTX - 1 - block) * HALF + offset


def episodes_of(x_ref, at, group):
    lane = lax.broadcasted_iota(jnp.int32, (1, ROWS), 1) // PIECE
    out = jnp.zeros((1, ROWS), f32)
    for u in range(4):
        rows = x_ref[4 * group + u, 3 * PIECE : 3 * PIECE + STAT, :].astype(f32)
        out = jnp.where(lane == u, rows[at : at + 1], out)
    return out


def split3(x):
    high = x.astype(bf16).astype(f32)
    rest = x - high
    mid = rest.astype(bf16).astype(f32)
    return high, mid, rest - mid


def stat_rows(a, b):
    row = lax.broadcasted_iota(jnp.int32, (STAT, ROWS), 0)
    out = jnp.zeros((STAT, ROWS), f32)
    for at, piece in enumerate(split3(a) + split3(b)):
        out = jnp.where(row == at, piece, out)
    return out


def stats_of(rows):
    return rows[0:1] + rows[1:2] + rows[2:3], rows[3:4] + rows[4:5] + rows[5:6]


def tile(rows, at):
    own = rows[:, at * PIECE : (at + 1) * PIECE]
    return jnp.concatenate([own] * 4, axis=1).astype(bf16)


def merge(pieces):
    lane = lax.broadcasted_iota(jnp.int32, (STAT, ROWS), 1) // PIECE
    out = jnp.zeros((STAT, ROWS), f32)
    for u, piece in enumerate(pieces):
        out = jnp.where(lane == u, piece.astype(f32), out)
    return out


def key_columns(pos_ref, x_ref, group):
    row = lax.broadcasted_iota(jnp.int32, (ROWS, ROWS), 0) + group * ROWS
    times = times_of(row, pos_ref[2] * 2 + pos_ref[1], pos_ref[3])
    return times, jnp.broadcast_to(episodes_of(x_ref, 1, group), (ROWS, ROWS)).T


def query_rows(pos_ref, x_ref, group):
    row = lax.broadcasted_iota(jnp.int32, (1, ROWS), 1) + group * ROWS
    times = times_of(row, pos_ref[0], pos_ref[3])
    return times, episodes_of(x_ref, 0, group) - WINDOW


def part(x_ref, at, first=0, count=SHARES):
    return x_ref[first : first + count, at * PIECE : (at + 1) * PIECE, :].reshape(count * PIECE, HD)


def prepare_kernel(q_ref, k_ref, v_ref, ep_ref, qkv_out, ep_buf, sems):
    copies = [
        pltpu.make_async_copy(q_ref, qkv_out.at[0:ROWS], sems.at[0]),
        pltpu.make_async_copy(k_ref, qkv_out.at[ROWS : 2 * ROWS], sems.at[1]),
        pltpu.make_async_copy(v_ref, qkv_out.at[2 * ROWS : 3 * ROWS], sems.at[2]),
        pltpu.make_async_copy(ep_ref, ep_buf, sems.at[3]),
    ]
    for copy in copies:
        copy.start()
    for copy in copies:
        copy.wait()
    ep = jnp.broadcast_to(ep_buf[...].astype(f32), (STAT, ROWS)).astype(bf16)
    qkv_out[3 * ROWS : 3 * ROWS + STAT] = jnp.concatenate([ep, ep], axis=1)


def repeat_kernel(d_ref, d_out, d_buf, sem):
    copy = pltpu.make_async_copy(d_ref, d_buf, sem)
    copy.start()
    copy.wait()
    for s in range(PLANES):
        d_out[s] = d_buf[...]


def pack_kernel(qkv_ref, out_ref):
    ep = qkv_ref[3 * ROWS : 3 * ROWS + STAT, 0:ROWS].astype(f32)
    tiled = []
    for piece in range(4):
        own = ep[:, piece * PIECE : (piece + 1) * PIECE]
        tiled.append(jnp.concatenate([own] * 4, axis=1))
    row = lax.broadcasted_iota(jnp.int32, (STAT, ROWS), 0)
    for xh in range(2):
        for y in range(4):
            for xl in range(2):
                x = xh * 2 + xl
                both = jnp.where(row == 0, tiled[y], tiled[x]).astype(bf16)
                for core in range(2):
                    s = share(xh, y, xl, core)
                    cols = slice(core * HD, (core + 1) * HD)
                    q_rows = slice(y * PIECE, (y + 1) * PIECE)
                    out_ref[s, 0:PIECE, :] = qkv_ref[q_rows, cols]
                    for at in (1, 2):
                        k_rows = slice(at * ROWS + x * PIECE, at * ROWS + (x + 1) * PIECE)
                        out_ref[s, at * PIECE : (at + 1) * PIECE, :] = qkv_ref[k_rows, cols]
                    out_ref[s, 3 * PIECE : 3 * PIECE + STAT, :] = both


def forward_kernel(pos_ref, x_ref, o_ref, tk_ref, ek_ref, vt_ref):
    for g in range(8):
        at = slice(g * ROWS, (g + 1) * ROWS)
        tk_ref[at, :], ek_ref[at, :] = key_columns(pos_ref, x_ref, g)
        vt_ref[:, at] = part(x_ref, 2, 4 * g, 4).T
    keys = part(x_ref, 1)
    for g in range(0, 8, 2):
        qb = part(x_ref, 0, 4 * g, 8)
        st = lax.dot_general(keys, qb, NT, preferred_element_type=f32)
        low = []
        for u in range(2):
            tq, eq = query_rows(pos_ref, x_ref, g + u)
            at = slice(u * ROWS, (u + 1) * ROWS)
            seen = (tk_ref[...] <= tq) & (ek_ref[...] > eq)
            sc = jnp.where(seen, st[:, at] * (SCALE * LOG2E), FLOOR)
            top = jnp.max(sc, axis=0, keepdims=True)
            p = jnp.exp2(sc - top)
            rows = stat_rows(top, jnp.sum(p, axis=0, keepdims=True))
            low.append(p.astype(bf16))
            for j in range(4):
                o_ref[4 * (g + u) + j, PIECE : PIECE + STAT, :] = tile(rows, j)
        o = jnp.dot(vt_ref[...], jnp.concatenate(low, axis=1), preferred_element_type=f32)
        for u in range(2):
            four = slice(4 * (g + u), 4 * (g + u) + 4)
            out = o[:, u * ROWS : (u + 1) * ROWS].T.astype(bf16)
            o_ref[four, 0:PIECE, :] = out.reshape(4, PIECE, HD)


def combine_kernel(o_ref, da_ref, attn_ref, das_ref):
    for core in range(2):
        cols = slice(core * HD, (core + 1) * HD)
        tops, sums, parts = [], [], []
        for x in range(4):
            slots = [share(x // 2, y, x % 2, core) for y in range(4)]
            top, total = stats_of(merge([o_ref[s, PIECE : PIECE + STAT, :] for s in slots]))
            tops.append(top)
            sums.append(total)
            parts.append(jnp.concatenate([o_ref[s, 0:PIECE, :] for s in slots], axis=0).astype(f32))
        top = functools.reduce(jnp.maximum, tops)
        weights = [jnp.exp2(t - top) for t in tops]
        total = sum(w * t for w, t in zip(weights, sums))
        low = sum(
            jnp.broadcast_to(w / total, (ROWS, ROWS)).T * o for w, o in zip(weights, parts)
        ).astype(bf16)
        attn_ref[:, cols] = low
        da = da_ref[:, cols]
        delta = jnp.sum((da.astype(f32) * low.astype(f32)).T, axis=0, keepdims=True)
        rows = stat_rows(top + jnp.log(total) * LOG2E, delta)
        for y in range(4):
            own = tile(rows, y)
            for x in range(4):
                s = share(x // 2, y, x % 2, core)
                das_ref[s, 0:PIECE, :] = da[y * PIECE : (y + 1) * PIECE]
                das_ref[s, PIECE : PIECE + STAT, :] = own


def backward_kernel(pos_ref, x_ref, d_ref, grad_ref, dq_acc):
    queries, d_attn = part(x_ref, 0), part(d_ref, 0)
    rows, stats = [], []
    for g in range(8):
        rows.append(query_rows(pos_ref, x_ref, g))
        stats.append(
            stats_of(merge([d_ref[4 * g + u, PIECE : PIECE + STAT, :] for u in range(4)]))
        )
    for g in range(0, 8, 2):
        kb, vb = part(x_ref, 1, 4 * g, 8), part(x_ref, 2, 4 * g, 8)
        st = lax.dot_general(kb, queries, NT, preferred_element_type=f32)
        dp = lax.dot_general(vb, d_attn, NT, preferred_element_type=f32)
        tk0, ek0 = key_columns(pos_ref, x_ref, g)
        tk1, ek1 = key_columns(pos_ref, x_ref, g + 1)
        tk = jnp.concatenate([tk0, tk1], axis=0)
        ek = jnp.concatenate([ek0, ek1], axis=0)
        p_low, ds_low = [], []
        for u in range(8):
            at = slice(u * ROWS, (u + 1) * ROWS)
            (tq, eq), (lse, delta) = rows[u], stats[u]
            seen = (tk <= tq) & (ek > eq)
            p = jnp.where(seen, jnp.exp2(st[:, at] * (SCALE * LOG2E) - lse), 0.0)
            p_low.append(p.astype(bf16))
            ds_low.append((p * (dp[:, at] - delta)).astype(bf16))
        probs = jnp.concatenate(p_low, axis=1)
        ds = jnp.concatenate(ds_low, axis=1)
        dv = jnp.dot(probs, d_attn, preferred_element_type=f32)
        dk = jnp.dot(ds, queries, preferred_element_type=f32)
        dq = jnp.dot(kb.T, ds, preferred_element_type=f32)
        if g == 0:
            dq_acc[...] = dq
        else:
            dq_acc[...] += dq
        for at, grad in ((1, dk), (2, dv)):
            grad_ref[4 * g : 4 * g + 8, at * PIECE : (at + 1) * PIECE, :] = grad.astype(
                bf16
            ).reshape(8, PIECE, HD)
    for g in range(8):
        at = slice(g * ROWS, (g + 1) * ROWS)
        four = slice(4 * g, 4 * g + 4)
        grad_ref[four, 0:PIECE, :] = dq_acc[:, at].T.astype(bf16).reshape(4, PIECE, HD)


def grads_kernel(grad_ref, out_ref):
    for core in range(2):
        cols = slice(core * HD, (core + 1) * HD)
        for i in range(4):
            over_x = [grad_ref[share(x // 2, i, x % 2, core), 0:PIECE].astype(f32) for x in range(4)]
            rows = slice(i * PIECE, (i + 1) * PIECE)
            out_ref[rows, cols] = (sum(over_x) * SCALE).astype(bf16)
            over_y = [grad_ref[share(i // 2, y, i % 2, core), PIECE:].astype(f32) for y in range(4)]
            both = sum(over_y)
            rows = slice(ROWS + i * PIECE, ROWS + (i + 1) * PIECE)
            out_ref[rows, cols] = (both[:PIECE] * SCALE).astype(bf16)
            rows = slice(2 * ROWS + i * PIECE, 2 * ROWS + (i + 1) * PIECE)
            out_ref[rows, cols] = both[PIECE:].astype(bf16)


VMEM = pl.BlockSpec(memory_space=pltpu.VMEM)
SMEM = pl.BlockSpec(memory_space=pltpu.SMEM)


HBM = pl.BlockSpec(memory_space=pltpu.HBM)


def call(kernel, outs, args, scratch=(), flops=0, smem=0, space=VMEM, limit=32):
    size = lambda a: functools.reduce(lambda x, y: x * y, a.shape) * a.dtype.itemsize
    return pl.pallas_call(
        kernel,
        out_shape=outs,
        in_specs=[SMEM] * smem + [space] * (len(args) - smem),
        out_specs=[VMEM] * len(outs),
        scratch_shapes=list(scratch),
        compiler_params=pltpu.CompilerParams(vmem_limit_bytes=limit * 1024 * 1024),
        cost_estimate=pl.CostEstimate(
            flops=flops, bytes_accessed=sum(map(size, (*args, *outs))), transcendentals=0
        ),
    )(*args)


def turns():
    inside, across, there = [], [], []
    for z in range(PLANES):
        for g in range(PLANES):
            plane = place_of(g)
            at = slot_of(plane ^ z)
            inside.append((z * PLANES + g, z * PLANES + at))
            across.append((z * PLANES + at, plane * PLANES + at))
            there.append((z * PLANES + g, plane * PLANES + at))
    return inside, across, there, [(b, a) for a, b in there]


def on_device(queries, keys, values, episode, out_weight, d_out):
    rows, width = queries.shape
    total = SHARES * PIECE
    inside, across, there, back = turns()
    move = lambda x, pairs: lax.ppermute(x, TURN, pairs)
    swap = functools.partial(lax.all_to_all, split_axis=0, concat_axis=0, tiled=True)
    low = lambda *shape: jax.ShapeDtypeStruct(shape, bf16)
    pos = jnp.stack([lax.axis_index(a) for a in ("y", "xl", "xh", "z")]).astype(jnp.int32)
    (qkv,) = call(
        prepare_kernel,
        [low(3 * rows + STAT, width)],
        (queries, keys, values, episode.reshape(1, rows)),
        [pltpu.VMEM((1, rows), jnp.int32), pltpu.SemaphoreType.DMA((4,))],
        space=HBM,
        limit=60,
    )
    (d_slots,) = call(
        repeat_kernel,
        [low(PLANES, *d_out.shape)],
        (d_out,),
        [pltpu.VMEM(d_out.shape, bf16), pltpu.SemaphoreType.DMA],
        space=HBM,
        limit=60,
    )
    qkv, d_slots = lax.optimization_barrier((move(qkv, inside), d_slots))
    qkv = move(qkv, across)
    d_out_all = swap(d_slots, HEAD)
    d_attn = lax.dot_general(
        d_out_all.reshape(rows, -1), out_weight, NT, preferred_element_type=f32
    ).astype(bf16)
    qkv, d_attn = lax.optimization_barrier((qkv, d_attn))
    d_attn = move(d_attn, there)
    (slots,) = call(pack_kernel, [low(SHARES, 3 * PIECE + STAT, HD)], (qkv,))
    held = swap(slots, PLANE)
    (o_slots,) = call(
        forward_kernel,
        [low(SHARES, PIECE + STAT, HD)],
        (pos, held),
        [
            pltpu.VMEM((total, ROWS), jnp.int32),
            pltpu.VMEM((total, ROWS), f32),
            pltpu.VMEM((HD, total), bf16),
        ],
        flops=4 * total * total * HD,
        smem=1,
    )
    o_slots, d_attn = lax.optimization_barrier((o_slots, d_attn))
    attn, da_slots = call(
        combine_kernel,
        [low(rows, width), low(SHARES, PIECE + STAT, HD)],
        (swap(o_slots, PLANE), d_attn),
    )
    attn = move(attn, back)
    (grad_slots,) = call(
        backward_kernel,
        [low(SHARES, 3 * PIECE, HD)],
        (pos, held, swap(da_slots, PLANE)),
        [pltpu.VMEM((HD, total), f32)],
        flops=10 * total * total * HD,
        smem=1,
    )
    grad_parts, attn = lax.optimization_barrier((swap(grad_slots, PLANE), attn))
    (grads,) = call(grads_kernel, [low(3 * rows, width)], (grad_parts,))
    grads = move(grads, back)
    partial = jnp.dot(attn, out_weight, preferred_element_type=f32).astype(bf16)
    parts = swap(partial.reshape((PLANES,) + d_out.shape), HEAD)
    mixed = jnp.sum(parts.astype(f32), axis=0).astype(bf16)
    return mixed, grads[:rows], grads[rows : 2 * rows], grads[2 * rows :]


def solution(mesh):
    inner = Mesh(mesh.devices.reshape(16, 2, 4, 2, 2), AXES)
    ctx = ("z", "xh")
    block = P(ctx, HEAD)
    whole = P(ctx + HEAD, None)
    return jax.shard_map(
        on_device,
        mesh=inner,
        in_specs=(block, block, block, P(ctx), P(HEAD, None), whole),
        out_specs=(whole, block, block, block),
        check_vma=False,
    )
```

```python
import functools

import jax
import jax.numpy as jnp
from jax import lax
from jax.experimental import pallas as pl
from jax.experimental.pallas import tpu as pltpu
from jax.sharding import Mesh, PartitionSpec as P

HD = 128
ROWS = 128
HALF = ROWS // 2
PIECE = 32
SHARES = 32
PLANES = 16
CTX = 32
WINDOW = 2 * CTX
STAT = 16
LOG2E = 1.4426950408889634
SCALE = HD ** (-0.5)
FLOOR = -1e30

AXES = ("z", "xh", "y", "xl", "core")
HEAD = ("y", "xl", "core")
TURN = ("z",) + HEAD
PLANE = ("xh",) + HEAD

f32 = jnp.float32
bf16 = jnp.bfloat16
NT = (((1,), (1,)), ((), ()))


def slot_of(place):
    return place % 8 * 2 + place // 8


def place_of(slot):
    return slot // 2 + slot % 2 * 8


def share(xh, y, xl, core):
    return ((xh * 4 + y) * 2 + xl) * 2 + core


def times_of(row, piece, plane):
    source = row // PIECE
    place = source % 2 * 8 + source // 4 % 4 * 2 + source // 2 % 2
    block = (place ^ plane) * 2 + source // 16
    offset = row % PIECE + piece % 2 * PIECE
    return jnp.where(piece < 2, block, 2 * CTX - 1 - block) * HALF + offset


def episodes_of(x_ref, at, group):
    lane = lax.broadcasted_iota(jnp.int32, (1, ROWS), 1) // PIECE
    out = jnp.zeros((1, ROWS), f32)
    for u in range(4):
        rows = x_ref[4 * group + u, 3 * PIECE : 3 * PIECE + STAT, :].astype(f32)
        out = jnp.where(lane == u, rows[at : at + 1], out)
    return out


def split3(x):
    high = x.astype(bf16).astype(f32)
    rest = x - high
    mid = rest.astype(bf16).astype(f32)
    return high, mid, rest - mid


def stat_rows(a, b):
    row = lax.broadcasted_iota(jnp.int32, (STAT, ROWS), 0)
    out = jnp.zeros((STAT, ROWS), f32)
    for at, piece in enumerate(split3(a) + split3(b)):
        out = jnp.where(row == at, piece, out)
    return out


def stats_of(rows):
    return rows[0:1] + rows[1:2] + rows[2:3], rows[3:4] + rows[4:5] + rows[5:6]


def tile(rows, at):
    own = rows[:, at * PIECE : (at + 1) * PIECE]
    return jnp.concatenate([own] * 4, axis=1).astype(bf16)


def merge(pieces):
    lane = lax.broadcasted_iota(jnp.int32, (STAT, ROWS), 1) // PIECE
    out = jnp.zeros((STAT, ROWS), f32)
    for u, piece in enumerate(pieces):
        out = jnp.where(lane == u, piece.astype(f32), out)
    return out


def key_columns(pos_ref, x_ref, group):
    row = lax.broadcasted_iota(jnp.int32, (ROWS, ROWS), 0) + group * ROWS
    times = times_of(row, pos_ref[2] * 2 + pos_ref[1], pos_ref[3])
    return times, jnp.broadcast_to(episodes_of(x_ref, 1, group), (ROWS, ROWS)).T


def query_rows(pos_ref, x_ref, group):
    row = lax.broadcasted_iota(jnp.int32, (1, ROWS), 1) + group * ROWS
    times = times_of(row, pos_ref[0], pos_ref[3])
    return times, episodes_of(x_ref, 0, group) - WINDOW


def part(x_ref, at, first=0, count=SHARES):
    return x_ref[first : first + count, at * PIECE : (at + 1) * PIECE, :].reshape(count * PIECE, HD)


def prepare_kernel(q_ref, k_ref, v_ref, ep_ref, qkv_out, ep_buf, sems):
    copies = [
        pltpu.make_async_copy(q_ref, qkv_out.at[0:ROWS], sems.at[0]),
        pltpu.make_async_copy(k_ref, qkv_out.at[ROWS : 2 * ROWS], sems.at[1]),
        pltpu.make_async_copy(v_ref, qkv_out.at[2 * ROWS : 3 * ROWS], sems.at[2]),
        pltpu.make_async_copy(ep_ref, ep_buf, sems.at[3]),
    ]
    for copy in copies:
        copy.start()
    for copy in copies:
        copy.wait()
    ep = jnp.broadcast_to(ep_buf[...].astype(f32), (STAT, ROWS)).astype(bf16)
    qkv_out[3 * ROWS : 3 * ROWS + STAT] = jnp.concatenate([ep, ep], axis=1)


def repeat_kernel(d_ref, d_out, d_buf, sem):
    copy = pltpu.make_async_copy(d_ref, d_buf, sem)
    copy.start()
    copy.wait()
    for s in range(PLANES):
        d_out[s] = d_buf[...]


def pack_kernel(qkv_ref, out_ref):
    ep = qkv_ref[3 * ROWS : 3 * ROWS + STAT, 0:ROWS].astype(f32)
    tiled = []
    for piece in range(4):
        own = ep[:, piece * PIECE : (piece + 1) * PIECE]
        tiled.append(jnp.concatenate([own] * 4, axis=1))
    row = lax.broadcasted_iota(jnp.int32, (STAT, ROWS), 0)
    for xh in range(2):
        for y in range(4):
            for xl in range(2):
                x = xh * 2 + xl
                both = jnp.where(row == 0, tiled[y], tiled[x]).astype(bf16)
                for core in range(2):
                    s = share(xh, y, xl, core)
                    cols = slice(core * HD, (core + 1) * HD)
                    q_rows = slice(y * PIECE, (y + 1) * PIECE)
                    out_ref[s, 0:PIECE, :] = qkv_ref[q_rows, cols]
                    for at in (1, 2):
                        k_rows = slice(at * ROWS + x * PIECE, at * ROWS + (x + 1) * PIECE)
                        out_ref[s, at * PIECE : (at + 1) * PIECE, :] = qkv_ref[k_rows, cols]
                    out_ref[s, 3 * PIECE : 3 * PIECE + STAT, :] = both


def forward_kernel(pos_ref, x_ref, o_ref, tk_ref, ek_ref, vt_ref):
    for g in range(8):
        at = slice(g * ROWS, (g + 1) * ROWS)
        tk_ref[at, :], ek_ref[at, :] = key_columns(pos_ref, x_ref, g)
        vt_ref[:, at] = part(x_ref, 2, 4 * g, 4).T
    keys = part(x_ref, 1)
    for g in range(0, 8, 2):
        qb = part(x_ref, 0, 4 * g, 8)
        st = lax.dot_general(keys, qb, NT, preferred_element_type=f32)
        low = []
        for u in range(2):
            tq, eq = query_rows(pos_ref, x_ref, g + u)
            at = slice(u * ROWS, (u + 1) * ROWS)
            seen = (tk_ref[...] <= tq) & (ek_ref[...] > eq)
            sc = jnp.where(seen, st[:, at] * (SCALE * LOG2E), FLOOR)
            top = jnp.max(sc, axis=0, keepdims=True)
            p = jnp.exp2(sc - top)
            rows = stat_rows(top, jnp.sum(p, axis=0, keepdims=True))
            low.append(p.astype(bf16))
            for j in range(4):
                o_ref[4 * (g + u) + j, PIECE : PIECE + STAT, :] = tile(rows, j)
        o = jnp.dot(vt_ref[...], jnp.concatenate(low, axis=1), preferred_element_type=f32)
        for u in range(2):
            four = slice(4 * (g + u), 4 * (g + u) + 4)
            out = o[:, u * ROWS : (u + 1) * ROWS].T.astype(bf16)
            o_ref[four, 0:PIECE, :] = out.reshape(4, PIECE, HD)


def combine_kernel(o_ref, da_ref, attn_ref, das_ref):
    for core in range(2):
        cols = slice(core * HD, (core + 1) * HD)
        tops, sums, parts = [], [], []
        for x in range(4):
            slots = [share(x // 2, y, x % 2, core) for y in range(4)]
            top, total = stats_of(merge([o_ref[s, PIECE : PIECE + STAT, :] for s in slots]))
            tops.append(top)
            sums.append(total)
            parts.append(jnp.concatenate([o_ref[s, 0:PIECE, :] for s in slots], axis=0).astype(f32))
        top = functools.reduce(jnp.maximum, tops)
        weights = [jnp.exp2(t - top) for t in tops]
        total = sum(w * t for w, t in zip(weights, sums))
        low = sum(
            jnp.broadcast_to(w / total, (ROWS, ROWS)).T * o for w, o in zip(weights, parts)
        ).astype(bf16)
        attn_ref[:, cols] = low
        da = da_ref[:, cols]
        delta = jnp.sum((da.astype(f32) * low.astype(f32)).T, axis=0, keepdims=True)
        rows = stat_rows(top + jnp.log(total) * LOG2E, delta)
        for y in range(4):
            own = tile(rows, y)
            for x in range(4):
                s = share(x // 2, y, x % 2, core)
                das_ref[s, 0:PIECE, :] = da[y * PIECE : (y + 1) * PIECE]
                das_ref[s, PIECE : PIECE + STAT, :] = own


def backward_kernel(pos_ref, x_ref, d_ref, grad_ref, dq_acc):
    queries, d_attn = part(x_ref, 0), part(d_ref, 0)
    rows, stats = [], []
    for g in range(8):
        rows.append(query_rows(pos_ref, x_ref, g))
        stats.append(
            stats_of(merge([d_ref[4 * g + u, PIECE : PIECE + STAT, :] for u in range(4)]))
        )
    for g in range(0, 8, 2):
        kb, vb = part(x_ref, 1, 4 * g, 8), part(x_ref, 2, 4 * g, 8)
        st = lax.dot_general(kb, queries, NT, preferred_element_type=f32)
        dp = lax.dot_general(vb, d_attn, NT, preferred_element_type=f32)
        tk0, ek0 = key_columns(pos_ref, x_ref, g)
        tk1, ek1 = key_columns(pos_ref, x_ref, g + 1)
        tk = jnp.concatenate([tk0, tk1], axis=0)
        ek = jnp.concatenate([ek0, ek1], axis=0)
        p_low, ds_low = [], []
        for u in range(8):
            at = slice(u * ROWS, (u + 1) * ROWS)
            (tq, eq), (lse, delta) = rows[u], stats[u]
            seen = (tk <= tq) & (ek > eq)
            p = jnp.where(seen, jnp.exp2(st[:, at] * (SCALE * LOG2E) - lse), 0.0)
            p_low.append(p.astype(bf16))
            ds_low.append((p * (dp[:, at] - delta)).astype(bf16))
        probs = jnp.concatenate(p_low, axis=1)
        ds = jnp.concatenate(ds_low, axis=1)
        dv = jnp.dot(probs, d_attn, preferred_element_type=f32)
        dk = jnp.dot(ds, queries, preferred_element_type=f32)
        dq = jnp.dot(kb.T, ds, preferred_element_type=f32)
        if g == 0:
            dq_acc[...] = dq
        else:
            dq_acc[...] += dq
        for at, grad in ((1, dk), (2, dv)):
            grad_ref[4 * g : 4 * g + 8, at * PIECE : (at + 1) * PIECE, :] = grad.astype(
                bf16
            ).reshape(8, PIECE, HD)
    for g in range(8):
        at = slice(g * ROWS, (g + 1) * ROWS)
        four = slice(4 * g, 4 * g + 4)
        grad_ref[four, 0:PIECE, :] = dq_acc[:, at].T.astype(bf16).reshape(4, PIECE, HD)


def grads_kernel(grad_ref, out_ref):
    for core in range(2):
        cols = slice(core * HD, (core + 1) * HD)
        for i in range(4):
            over_x = [grad_ref[share(x // 2, i, x % 2, core), 0:PIECE].astype(f32) for x in range(4)]
            rows = slice(i * PIECE, (i + 1) * PIECE)
            out_ref[rows, cols] = (sum(over_x) * SCALE).astype(bf16)
            over_y = [grad_ref[share(i // 2, y, i % 2, core), PIECE:].astype(f32) for y in range(4)]
            both = sum(over_y)
            rows = slice(ROWS + i * PIECE, ROWS + (i + 1) * PIECE)
            out_ref[rows, cols] = (both[:PIECE] * SCALE).astype(bf16)
            rows = slice(2 * ROWS + i * PIECE, 2 * ROWS + (i + 1) * PIECE)
            out_ref[rows, cols] = both[PIECE:].astype(bf16)


VMEM = pl.BlockSpec(memory_space=pltpu.VMEM)
SMEM = pl.BlockSpec(memory_space=pltpu.SMEM)


HBM = pl.BlockSpec(memory_space=pltpu.HBM)


def call(kernel, outs, args, scratch=(), flops=0, smem=0, space=VMEM, limit=32):
    size = lambda a: functools.reduce(lambda x, y: x * y, a.shape) * a.dtype.itemsize
    return pl.pallas_call(
        kernel,
        out_shape=outs,
        in_specs=[SMEM] * smem + [space] * (len(args) - smem),
        out_specs=[VMEM] * len(outs),
        scratch_shapes=list(scratch),
        compiler_params=pltpu.CompilerParams(vmem_limit_bytes=limit * 1024 * 1024),
        cost_estimate=pl.CostEstimate(
            flops=flops, bytes_accessed=sum(map(size, (*args, *outs))), transcendentals=0
        ),
    )(*args)


def turns():
    inside, across, there = [], [], []
    for z in range(PLANES):
        for g in range(PLANES):
            plane = place_of(g)
            at = slot_of(plane ^ z)
            inside.append((z * PLANES + g, z * PLANES + at))
            across.append((z * PLANES + at, plane * PLANES + at))
            there.append((z * PLANES + g, plane * PLANES + at))
    return inside, across, there, [(b, a) for a, b in there]


def on_device(queries, keys, values, episode, out_weight, d_out):
    rows, width = queries.shape
    total = SHARES * PIECE
    inside, across, there, back = turns()
    move = lambda x, pairs: lax.ppermute(x, TURN, pairs)
    swap = functools.partial(lax.all_to_all, split_axis=0, concat_axis=0, tiled=True)
    low = lambda *shape: jax.ShapeDtypeStruct(shape, bf16)
    pos = jnp.stack([lax.axis_index(a) for a in ("y", "xl", "xh", "z")]).astype(jnp.int32)
    (qkv,) = call(
        prepare_kernel,
        [low(3 * rows + STAT, width)],
        (queries, keys, values, episode.reshape(1, rows)),
        [pltpu.VMEM((1, rows), jnp.int32), pltpu.SemaphoreType.DMA((4,))],
        space=HBM,
        limit=60,
    )
    (d_slots,) = call(
        repeat_kernel,
        [low(PLANES, *d_out.shape)],
        (d_out,),
        [pltpu.VMEM(d_out.shape, bf16), pltpu.SemaphoreType.DMA],
        space=HBM,
        limit=60,
    )
    qkv, d_slots = lax.optimization_barrier((move(qkv, inside), d_slots))
    qkv = move(qkv, across)
    d_out_all = swap(d_slots, HEAD)
    d_attn = lax.dot_general(
        d_out_all.reshape(rows, -1), out_weight, NT, preferred_element_type=f32
    ).astype(bf16)
    qkv, d_attn = lax.optimization_barrier((qkv, d_attn))
    d_attn = move(d_attn, there)
    (slots,) = call(pack_kernel, [low(SHARES, 3 * PIECE + STAT, HD)], (qkv,))
    held = swap(slots, PLANE)
    (o_slots,) = call(
        forward_kernel,
        [low(SHARES, PIECE + STAT, HD)],
        (pos, held),
        [
            pltpu.VMEM((total, ROWS), jnp.int32),
            pltpu.VMEM((total, ROWS), f32),
            pltpu.VMEM((HD, total), bf16),
        ],
        flops=4 * total * total * HD,
        smem=1,
    )
    o_slots, d_attn = lax.optimization_barrier((o_slots, d_attn))
    attn, da_slots = call(
        combine_kernel,
        [low(rows, width), low(SHARES, PIECE + STAT, HD)],
        (swap(o_slots, PLANE), d_attn),
    )
    attn = move(attn, back)
    (grad_slots,) = call(
        backward_kernel,
        [low(SHARES, 3 * PIECE, HD)],
        (pos, held, swap(da_slots, PLANE)),
        [pltpu.VMEM((HD, total), f32)],
        flops=10 * total * total * HD,
        smem=1,
    )
    grad_slots, attn = lax.optimization_barrier((grad_slots, attn))
    (grads,) = call(grads_kernel, [low(3 * rows, width)], (swap(grad_slots, PLANE),))
    grads = move(grads, back)
    partial = jnp.dot(attn, out_weight, preferred_element_type=f32).astype(bf16)
    parts = swap(partial.reshape((PLANES,) + d_out.shape), HEAD)
    mixed = jnp.sum(parts.astype(f32), axis=0).astype(bf16)
    return mixed, grads[:rows], grads[rows : 2 * rows], grads[2 * rows :]


def solution(mesh):
    inner = Mesh(mesh.devices.reshape(16, 2, 4, 2, 2), AXES)
    ctx = ("z", "xh")
    block = P(ctx, HEAD)
    whole = P(ctx + HEAD, None)
    return jax.shard_map(
        on_device,
        mesh=inner,
        in_specs=(block, block, block, P(ctx), P(HEAD, None), whole),
        out_specs=(whole, block, block, block),
        check_vma=False,
    )
```

```python
import functools

import jax
import jax.numpy as jnp
from jax import lax
from jax.experimental import pallas as pl
from jax.experimental.pallas import tpu as pltpu
from jax.sharding import Mesh, PartitionSpec as P

HD = 128
ROWS = 128
HALF = ROWS // 2
PIECE = 32
SHARES = 32
PLANES = 16
CTX = 32
WINDOW = 2 * CTX
STAT = 16
LOG2E = 1.4426950408889634
SCALE = HD ** (-0.5)
FLOOR = -1e30

AXES = ("z", "xh", "y", "xl", "core")
HEAD = ("y", "xl", "core")
TURN = ("z",) + HEAD
PLANE = ("xh",) + HEAD

f32 = jnp.float32
bf16 = jnp.bfloat16
NT = (((1,), (1,)), ((), ()))


def slot_of(place):
    return place % 8 * 2 + place // 8


def place_of(slot):
    return slot // 2 + slot % 2 * 8


def share(xh, y, xl, core):
    return ((xh * 4 + y) * 2 + xl) * 2 + core


def times_of(row, piece, plane):
    source = row // PIECE
    place = source % 2 * 8 + source // 4 % 4 * 2 + source // 2 % 2
    block = (place ^ plane) * 2 + source // 16
    offset = row % PIECE + piece % 2 * PIECE
    return jnp.where(piece < 2, block, 2 * CTX - 1 - block) * HALF + offset


def episodes_of(x_ref, at, group):
    lane = lax.broadcasted_iota(jnp.int32, (1, ROWS), 1) // PIECE
    out = jnp.zeros((1, ROWS), f32)
    for u in range(4):
        rows = x_ref[4 * group + u, 3 * PIECE : 3 * PIECE + STAT, :].astype(f32)
        out = jnp.where(lane == u, rows[at : at + 1], out)
    return out


def split3(x):
    high = x.astype(bf16).astype(f32)
    rest = x - high
    mid = rest.astype(bf16).astype(f32)
    return high, mid, rest - mid


def stat_rows(a, b):
    row = lax.broadcasted_iota(jnp.int32, (STAT, ROWS), 0)
    out = jnp.zeros((STAT, ROWS), f32)
    for at, piece in enumerate(split3(a) + split3(b)):
        out = jnp.where(row == at, piece, out)
    return out


def stats_of(rows):
    return rows[0:1] + rows[1:2] + rows[2:3], rows[3:4] + rows[4:5] + rows[5:6]


def tile(rows, at):
    own = rows[:, at * PIECE : (at + 1) * PIECE]
    return jnp.concatenate([own] * 4, axis=1).astype(bf16)


def merge(pieces):
    lane = lax.broadcasted_iota(jnp.int32, (STAT, ROWS), 1) // PIECE
    out = jnp.zeros((STAT, ROWS), f32)
    for u, piece in enumerate(pieces):
        out = jnp.where(lane == u, piece.astype(f32), out)
    return out


def key_columns(pos_ref, x_ref, group):
    row = lax.broadcasted_iota(jnp.int32, (ROWS, ROWS), 0) + group * ROWS
    times = times_of(row, pos_ref[2] * 2 + pos_ref[1], pos_ref[3])
    return times, jnp.broadcast_to(episodes_of(x_ref, 1, group), (ROWS, ROWS)).T


def query_rows(pos_ref, x_ref, group):
    row = lax.broadcasted_iota(jnp.int32, (1, ROWS), 1) + group * ROWS
    times = times_of(row, pos_ref[0], pos_ref[3])
    return times, episodes_of(x_ref, 0, group) - WINDOW


def part(x_ref, at, first=0, count=SHARES):
    return x_ref[first : first + count, at * PIECE : (at + 1) * PIECE, :].reshape(count * PIECE, HD)


def prepare_kernel(q_ref, k_ref, v_ref, ep_ref, qkv_out, ep_buf, sems):
    copies = [
        pltpu.make_async_copy(q_ref, qkv_out.at[0:ROWS], sems.at[0]),
        pltpu.make_async_copy(k_ref, qkv_out.at[ROWS : 2 * ROWS], sems.at[1]),
        pltpu.make_async_copy(v_ref, qkv_out.at[2 * ROWS : 3 * ROWS], sems.at[2]),
        pltpu.make_async_copy(ep_ref, ep_buf, sems.at[3]),
    ]
    for copy in copies:
        copy.start()
    for copy in copies:
        copy.wait()
    ep = jnp.broadcast_to(ep_buf[...].astype(f32), (STAT, ROWS)).astype(bf16)
    qkv_out[3 * ROWS : 3 * ROWS + STAT] = jnp.concatenate([ep, ep], axis=1)


def repeat_kernel(d_ref, d_out, d_buf, sem):
    copy = pltpu.make_async_copy(d_ref, d_buf, sem)
    copy.start()
    copy.wait()
    for s in range(PLANES):
        d_out[s] = d_buf[...]


def pack_kernel(qkv_ref, out_ref):
    ep = qkv_ref[3 * ROWS : 3 * ROWS + STAT, 0:ROWS].astype(f32)
    tiled = []
    for piece in range(4):
        own = ep[:, piece * PIECE : (piece + 1) * PIECE]
        tiled.append(jnp.concatenate([own] * 4, axis=1))
    row = lax.broadcasted_iota(jnp.int32, (STAT, ROWS), 0)
    for xh in range(2):
        for y in range(4):
            for xl in range(2):
                x = xh * 2 + xl
                both = jnp.where(row == 0, tiled[y], tiled[x]).astype(bf16)
                for core in range(2):
                    s = share(xh, y, xl, core)
                    cols = slice(core * HD, (core + 1) * HD)
                    q_rows = slice(y * PIECE, (y + 1) * PIECE)
                    out_ref[s, 0:PIECE, :] = qkv_ref[q_rows, cols]
                    for at in (1, 2):
                        k_rows = slice(at * ROWS + x * PIECE, at * ROWS + (x + 1) * PIECE)
                        out_ref[s, at * PIECE : (at + 1) * PIECE, :] = qkv_ref[k_rows, cols]
                    out_ref[s, 3 * PIECE : 3 * PIECE + STAT, :] = both


def forward_kernel(pos_ref, x_ref, o_ref, tk_ref, ek_ref, vt_ref):
    for g in range(8):
        at = slice(g * ROWS, (g + 1) * ROWS)
        tk_ref[at, :], ek_ref[at, :] = key_columns(pos_ref, x_ref, g)
        vt_ref[:, at] = part(x_ref, 2, 4 * g, 4).T
    keys = part(x_ref, 1)
    for g in range(0, 8, 2):
        qb = part(x_ref, 0, 4 * g, 8)
        st = lax.dot_general(keys, qb, NT, preferred_element_type=f32)
        low = []
        for u in range(2):
            tq, eq = query_rows(pos_ref, x_ref, g + u)
            at = slice(u * ROWS, (u + 1) * ROWS)
            seen = (tk_ref[...] <= tq) & (ek_ref[...] > eq)
            sc = jnp.where(seen, st[:, at] * (SCALE * LOG2E), FLOOR)
            top = jnp.max(sc, axis=0, keepdims=True)
            p = jnp.exp2(sc - top)
            rows = stat_rows(top, jnp.sum(p, axis=0, keepdims=True))
            low.append(p.astype(bf16))
            for j in range(4):
                o_ref[4 * (g + u) + j, PIECE : PIECE + STAT, :] = tile(rows, j)
        o = jnp.dot(vt_ref[...], jnp.concatenate(low, axis=1), preferred_element_type=f32)
        for u in range(2):
            four = slice(4 * (g + u), 4 * (g + u) + 4)
            out = o[:, u * ROWS : (u + 1) * ROWS].T.astype(bf16)
            o_ref[four, 0:PIECE, :] = out.reshape(4, PIECE, HD)


def combine_kernel(o_ref, da_ref, attn_ref, das_ref):
    for core in range(2):
        cols = slice(core * HD, (core + 1) * HD)
        tops, sums, parts = [], [], []
        for x in range(4):
            slots = [share(x // 2, y, x % 2, core) for y in range(4)]
            top, total = stats_of(merge([o_ref[s, PIECE : PIECE + STAT, :] for s in slots]))
            tops.append(top)
            sums.append(total)
            parts.append(jnp.concatenate([o_ref[s, 0:PIECE, :] for s in slots], axis=0).astype(f32))
        top = functools.reduce(jnp.maximum, tops)
        weights = [jnp.exp2(t - top) for t in tops]
        total = sum(w * t for w, t in zip(weights, sums))
        low = sum(
            jnp.broadcast_to(w / total, (ROWS, ROWS)).T * o for w, o in zip(weights, parts)
        ).astype(bf16)
        attn_ref[:, cols] = low
        da = da_ref[:, cols]
        delta = jnp.sum((da.astype(f32) * low.astype(f32)).T, axis=0, keepdims=True)
        rows = stat_rows(top + jnp.log(total) * LOG2E, delta)
        for y in range(4):
            own = tile(rows, y)
            for x in range(4):
                s = share(x // 2, y, x % 2, core)
                das_ref[s, 0:PIECE, :] = da[y * PIECE : (y + 1) * PIECE]
                das_ref[s, PIECE : PIECE + STAT, :] = own


def backward_kernel(pos_ref, x_ref, d_ref, grad_ref, dq_acc):
    queries, d_attn = part(x_ref, 0), part(d_ref, 0)
    rows, stats = [], []
    for g in range(8):
        rows.append(query_rows(pos_ref, x_ref, g))
        stats.append(
            stats_of(merge([d_ref[4 * g + u, PIECE : PIECE + STAT, :] for u in range(4)]))
        )
    for g in range(0, 8, 2):
        kb, vb = part(x_ref, 1, 4 * g, 8), part(x_ref, 2, 4 * g, 8)
        st = lax.dot_general(kb, queries, NT, preferred_element_type=f32)
        dp = lax.dot_general(vb, d_attn, NT, preferred_element_type=f32)
        tk0, ek0 = key_columns(pos_ref, x_ref, g)
        tk1, ek1 = key_columns(pos_ref, x_ref, g + 1)
        tk = jnp.concatenate([tk0, tk1], axis=0)
        ek = jnp.concatenate([ek0, ek1], axis=0)
        p_low, ds_low = [], []
        for u in range(8):
            at = slice(u * ROWS, (u + 1) * ROWS)
            (tq, eq), (lse, delta) = rows[u], stats[u]
            seen = (tk <= tq) & (ek > eq)
            p = jnp.where(seen, jnp.exp2(st[:, at] * (SCALE * LOG2E) - lse), 0.0)
            p_low.append(p.astype(bf16))
            ds_low.append((p * (dp[:, at] - delta)).astype(bf16))
        probs = jnp.concatenate(p_low, axis=1)
        ds = jnp.concatenate(ds_low, axis=1)
        dv = jnp.dot(probs, d_attn, preferred_element_type=f32)
        dk = jnp.dot(ds, queries, preferred_element_type=f32)
        dq = jnp.dot(kb.T, ds, preferred_element_type=f32)
        if g == 0:
            dq_acc[...] = dq
        else:
            dq_acc[...] += dq
        for at, grad in ((1, dk), (2, dv)):
            grad_ref[4 * g : 4 * g + 8, at * PIECE : (at + 1) * PIECE, :] = grad.astype(
                bf16
            ).reshape(8, PIECE, HD)
    for g in range(8):
        at = slice(g * ROWS, (g + 1) * ROWS)
        four = slice(4 * g, 4 * g + 4)
        grad_ref[four, 0:PIECE, :] = dq_acc[:, at].T.astype(bf16).reshape(4, PIECE, HD)


def grads_kernel(grad_ref, out_ref):
    for core in range(2):
        cols = slice(core * HD, (core + 1) * HD)
        for i in range(4):
            over_x = [grad_ref[share(x // 2, i, x % 2, core), 0:PIECE].astype(f32) for x in range(4)]
            rows = slice(i * PIECE, (i + 1) * PIECE)
            out_ref[rows, cols] = (sum(over_x) * SCALE).astype(bf16)
            over_y = [grad_ref[share(i // 2, y, i % 2, core), PIECE:].astype(f32) for y in range(4)]
            both = sum(over_y)
            rows = slice(ROWS + i * PIECE, ROWS + (i + 1) * PIECE)
            out_ref[rows, cols] = (both[:PIECE] * SCALE).astype(bf16)
            rows = slice(2 * ROWS + i * PIECE, 2 * ROWS + (i + 1) * PIECE)
            out_ref[rows, cols] = both[PIECE:].astype(bf16)


def mixed_kernel(x_ref, out_ref, buf, sem):
    copy = pltpu.make_async_copy(x_ref, buf, sem)
    copy.start()
    copy.wait()
    for c in range(0, buf.shape[1], 512):
        parts = buf[:, c : c + 512].astype(f32).reshape(PLANES, 8, 512)
        out_ref[:, c : c + 512] = jnp.sum(parts, axis=0).astype(bf16)


VMEM = pl.BlockSpec(memory_space=pltpu.VMEM)
SMEM = pl.BlockSpec(memory_space=pltpu.SMEM)


HBM = pl.BlockSpec(memory_space=pltpu.HBM)


def call(kernel, outs, args, scratch=(), flops=0, smem=0, space=VMEM, limit=32):
    size = lambda a: functools.reduce(lambda x, y: x * y, a.shape) * a.dtype.itemsize
    return pl.pallas_call(
        kernel,
        out_shape=outs,
        in_specs=[SMEM] * smem + [space] * (len(args) - smem),
        out_specs=[VMEM] * len(outs),
        scratch_shapes=list(scratch),
        compiler_params=pltpu.CompilerParams(vmem_limit_bytes=limit * 1024 * 1024),
        cost_estimate=pl.CostEstimate(
            flops=flops, bytes_accessed=sum(map(size, (*args, *outs))), transcendentals=0
        ),
    )(*args)


def turns():
    inside, across, there = [], [], []
    for z in range(PLANES):
        for g in range(PLANES):
            plane = place_of(g)
            at = slot_of(plane ^ z)
            inside.append((z * PLANES + g, z * PLANES + at))
            across.append((z * PLANES + at, plane * PLANES + at))
            there.append((z * PLANES + g, plane * PLANES + at))
    return inside, across, there, [(b, a) for a, b in there]


def on_device(queries, keys, values, episode, out_weight, d_out):
    rows, width = queries.shape
    total = SHARES * PIECE
    inside, across, there, back = turns()
    move = lambda x, pairs: lax.ppermute(x, TURN, pairs)
    swap = functools.partial(lax.all_to_all, split_axis=0, concat_axis=0, tiled=True)
    low = lambda *shape: jax.ShapeDtypeStruct(shape, bf16)
    pos = jnp.stack([lax.axis_index(a) for a in ("y", "xl", "xh", "z")]).astype(jnp.int32)
    (qkv,) = call(
        prepare_kernel,
        [low(3 * rows + STAT, width)],
        (queries, keys, values, episode.reshape(1, rows)),
        [pltpu.VMEM((1, rows), jnp.int32), pltpu.SemaphoreType.DMA((4,))],
        space=HBM,
        limit=60,
    )
    (d_slots,) = call(
        repeat_kernel,
        [low(PLANES, *d_out.shape)],
        (d_out,),
        [pltpu.VMEM(d_out.shape, bf16), pltpu.SemaphoreType.DMA],
        space=HBM,
        limit=60,
    )
    qkv, d_slots = lax.optimization_barrier((move(qkv, inside), d_slots))
    qkv = move(qkv, across)
    d_out_all = swap(d_slots, HEAD)
    d_attn = lax.dot_general(
        d_out_all.reshape(rows, -1), out_weight, NT, preferred_element_type=f32
    ).astype(bf16)
    d_attn = move(d_attn, there)
    (slots,) = call(pack_kernel, [low(SHARES, 3 * PIECE + STAT, HD)], (qkv,))
    held = swap(slots, PLANE)
    (o_slots,) = call(
        forward_kernel,
        [low(SHARES, PIECE + STAT, HD)],
        (pos, held),
        [
            pltpu.VMEM((total, ROWS), jnp.int32),
            pltpu.VMEM((total, ROWS), f32),
            pltpu.VMEM((HD, total), bf16),
        ],
        flops=4 * total * total * HD,
        smem=1,
    )
    o_slots, d_attn = lax.optimization_barrier((o_slots, d_attn))
    attn, da_slots = call(
        combine_kernel,
        [low(rows, width), low(SHARES, PIECE + STAT, HD)],
        (swap(o_slots, PLANE), d_attn),
    )
    attn = move(attn, back)
    (grad_slots,) = call(
        backward_kernel,
        [low(SHARES, 3 * PIECE, HD)],
        (pos, held, swap(da_slots, PLANE)),
        [pltpu.VMEM((HD, total), f32)],
        flops=10 * total * total * HD,
        smem=1,
    )
    grad_parts, attn = lax.optimization_barrier((swap(grad_slots, PLANE), attn))
    (grads,) = call(grads_kernel, [low(3 * rows, width)], (grad_parts,))
    grads = move(grads, back)
    partial = jnp.dot(attn, out_weight, preferred_element_type=f32).astype(bf16)
    parts = swap(partial.reshape((PLANES,) + d_out.shape), HEAD)
    (mixed,) = call(
        mixed_kernel,
        [low(*d_out.shape)],
        (parts.reshape(rows, -1),),
        [pltpu.VMEM((rows, d_out.shape[1]), bf16), pltpu.SemaphoreType.DMA],
        space=HBM,
        limit=60,
    )
    return mixed, grads[:rows], grads[rows : 2 * rows], grads[2 * rows :]


def solution(mesh):
    inner = Mesh(mesh.devices.reshape(16, 2, 4, 2, 2), AXES)
    ctx = ("z", "xh")
    block = P(ctx, HEAD)
    whole = P(ctx + HEAD, None)
    return jax.shard_map(
        on_device,
        mesh=inner,
        in_specs=(block, block, block, P(ctx), P(HEAD, None), whole),
        out_specs=(whole, block, block, block),
        check_vma=False,
    )
```
